32 devices in a mesh: seq: 8 (over y, x, core), fsdp: 4 (over z).
Axes of the slice: x: 2, y: 2, z: 4, core: 2. Of those that a mesh axis runs over, the one named last changes fastest.
Arguments:
- hidden_in: bfloat16 [4, 1024, 2880], P('fsdp', 'seq'), may hold values from -6 to 6
- out_grad: bfloat16 [4, 1024, 2880], P('fsdp', 'seq'), may hold values from -6 to 6
- boundary: int32 [4], P('fsdp'), may hold values from 1024 to 1024, as said below
- routes: int32 [4, 1024, 4], P('fsdp', 'seq'), may hold values from 0 to 7, all different within a row; in each aligned block of 128 rows (0 to 127, 128 to 255, ..., all dimensions but the last counted through in order) at most 72 rows name the same one
- gain_one: bfloat16 [2880], P('fsdp'), may hold values from 0.5 to 1.5
- w_query: bfloat16 [2880, 4096], P('fsdp'), may hold values from -0.109375 to 0.109375
- w_key: bfloat16 [2880, 512], P('fsdp'), may hold values from -0.109375 to 0.109375
- w_value: bfloat16 [2880, 512], P('fsdp'), may hold values from -0.109375 to 0.109375
- w_output: bfloat16 [4096, 2880], P('fsdp'), may hold values from -0.5 to 0.5
- sink_logits: bfloat16 [64], P('fsdp'), may hold values from 2 to 5
- gain_two: bfloat16 [2880], P('fsdp'), may hold values from 0.5 to 1.5
- w_router: bfloat16 [2880, 8], P('fsdp'), may hold values from -0.21875 to 0.21875
- w_in: bfloat16 [8, 2880, 5760], P('seq', 'fsdp'), may hold values from -0.25 to 0.25
- w_out: bfloat16 [8, 2880, 2880], P('seq', 'fsdp'), may hold values from -0.02734375 to 0.02734375
Outputs:
- block_out: bfloat16 [4, 1024, 2880], P('fsdp', 'seq')
- input_grad: float32 [4, 1024, 2880], P('fsdp', 'seq')
- grad_gain_one: float32 [2880], P('fsdp')
- grad_query: float32 [2880, 4096], P('fsdp')
- grad_key: float32 [2880, 512], P('fsdp')
- grad_value: float32 [2880, 512], P('fsdp')
- grad_output: float32 [4096, 2880], P('fsdp')
- grad_sinks: float32 [64], P('fsdp')
- grad_gain_two: float32 [2880], P('fsdp')
- grad_router: float32 [2880, 8], P('fsdp')
- grad_expert_in: float32 [8, 2880, 5760], P('seq', 'fsdp')
- grad_expert_out: float32 [8, 2880, 2880], P('seq', 'fsdp')
The draws below stay inside these ranges and needn't reach their ends.
Inputs may be any that keep to these rules, and one draw needn't show every extreme that they name: `routes`: each row names 4 different experts. Among the rows of one device (aligned blocks of 128 tokens), no expert is named more than 72 times, a bound that some block reaches. `boundary`: the longest sequence of every group has at least min(1024, 1024) tokens or half the group; group 0 holds one sequence.
All inputs are finite; a program needn't handle non-finite values.
Results may differ from the reference program's by a relative error of at most 0.028.
Values may be sent and summed in bfloat16 or wider, within the bound.
No kernel may reach another device: no remote copies, remote signals or barrier semaphores. Data moves between devices by JAX's collectives and lax.ppermute only.
A program may use at most 512 MiB of HBM per device.

```python
import math
import jax
import jax.numpy as jnp
import numpy as np
from jax import lax

D = 2880
HEADS = 64
KVH = 8
HD = 64
FF = 2880
TOP = 4
WIN = 128
TOK_DEV = 128
SEQ_LONG = 1024
EXPERTS = 8
SEQ_TOK = 1024
GROUPS = 4
CAP = 72


def draw_boundary(key, part):
    lower = max(SEQ_TOK // 2, min(SEQ_LONG, SEQ_TOK))
    values = jax.random.randint(key, (GROUPS,), lower, SEQ_TOK + 1, dtype=jnp.int32)
    values = values.at[0].set(SEQ_TOK)
    values = values.at[1].set(lower)
    return values.astype(jnp.int32)


def block_levels(rng, shape, shards, least, top_value):
    loudness, own = 1.0, jax.random.fold_in(rng, 6)
    for axis_at, blocks in shards:
        heights = jnp.exp(jax.random.uniform(jax.random.fold_in(own, axis_at), (blocks,), jnp.float32, least / len(shards), top_value / len(shards)))
        loudness = loudness * jnp.repeat(heights, shape[axis_at] // blocks).reshape([-1 if axis == axis_at else 1 for axis in range(len(shape))])
    return loudness


def assign_block(stream_key, own, number, rows, number_of, top, most, slope):
    ranking = jax.random.permutation(stream_key, number_of)
    crowded, ordinary = shares(number_of, rows * top, most, slope, True), shares(number_of, rows * top, most, slope, False)
    places = jnp.arange(number_of)

    def named(lengths, turn):
        used = int((lengths > 0).sum())
        fixed = max(1, used // 4)
        passed = fixed + (places - fixed + turn * (used - fixed)) % max(1, number_of - fixed)
        return jnp.zeros((number_of,), jnp.int32).at[ranking[jnp.where(places < fixed, places, passed)]].set(jnp.asarray(lengths, jnp.int32))

    lengths = jnp.where(number % 4 == 0, named(crowded, number // 4), named(ordinary, number - number // 4 - 1))
    mixed = jax.random.permutation(jax.random.fold_in(own, 3), number_of)
    giver, taker = mixed[0:number_of // 2 * 2:2], mixed[1:number_of // 2 * 2:2]
    slack = jnp.minimum(lengths[giver] - 1, most - lengths[taker]) // 2
    slack = jnp.where((giver == ranking[0]) | (taker == ranking[0]) | (lengths[taker] == 0), 0, jnp.maximum(slack, 0))
    passed = jax.random.randint(jax.random.fold_in(own, 4), (number_of // 2,), 0, 1 << 20) % (slack + 1)
    lengths = lengths.at[giver].add(-passed).at[taker].add(passed)
    members = jnp.searchsorted(jnp.cumsum(lengths), jnp.arange(rows * top), side="right").astype(jnp.int32)
    listing = members.reshape(top, rows).T
    listing = listing[jax.random.permutation(jax.random.fold_in(own, 1), rows)]
    turn = jax.random.randint(jax.random.fold_in(own, 2), (rows, 1), 0, top)
    return jnp.take_along_axis(listing, (jnp.arange(top)[None, :] + turn) % top, axis=1)


def shares(count, total, most, skew, full):
    portions = [(1 << 20) // math.isqrt(grade ** skew) + 1 for grade in range(1, count + 1)]
    largest = most if full else min(most, max(-(-total // count), total * portions[0] // sum(portions)))
    least = 1 if total - largest >= count - 1 else 0
    holding, surplus = [largest] + [least] * (count - 1), total - largest - least * (count - 1)
    while surplus > 0:
        free = [i for i in range(1, count) if holding[i] < largest] or [i for i in range(1, count) if holding[i] < most]
        mass, remaining = sum([portions[i] for i in free]), surplus
        for i in free:
            addition = min(most - holding[i], max(1, remaining * portions[i] // mass), surplus)
            holding[i] = holding[i] + addition
            surplus = surplus - addition
    return np.array(holding)


def scatter_about(stream_key, extent, width, limit, cuts=(), held_as=jnp.bfloat16):
    level = block_levels(stream_key, extent, cuts, -0.22, 0.18) if cuts else 1.0
    values = jax.random.normal(stream_key, extent, jnp.float32) * width * level
    return jnp.minimum(jnp.maximum(values, -limit), limit).astype(held_as)


def setup_inputs(seed: int = 0) -> dict:
    key_list = jax.random.split(jax.random.key(seed), 15)
    hidden_in = scatter_about(key_list[0], (GROUPS, SEQ_TOK, D), 1.0, 6.0, ((0, 4), (1, 8)))
    out_grad = scatter_about(key_list[1], (GROUPS, SEQ_TOK, D), 1.0, 6.0, ((0, 4), (1, 8)))
    boundary = draw_boundary(jax.random.fold_in(key_list[14], 71), 0)
    routes_keys = jax.random.split(jax.random.fold_in(key_list[3], 1), GROUPS * SEQ_TOK // TOK_DEV)
    routes_turns = jax.random.permutation(jax.random.fold_in(key_list[3], 3), GROUPS * SEQ_TOK // TOK_DEV)
    routes = jax.vmap(lambda own, number: assign_block(jax.random.fold_in(key_list[3], 2), own, number, TOK_DEV, EXPERTS, TOP, CAP, 2))(routes_keys, routes_turns).reshape((GROUPS, SEQ_TOK, TOP))
    gain_one = jnp.clip(1.0 + 0.1 * jax.random.normal(key_list[4], (D,), jnp.float32), 0.5, 1.5).astype(jnp.bfloat16)
    w_query = scatter_about(key_list[5], (D, HEADS * HD), D ** -0.5, 0.109375, ((0, 4),))
    w_key = scatter_about(key_list[6], (D, KVH * HD), D ** -0.5, 0.109375, ((0, 4),))
    w_value = scatter_about(key_list[7], (D, KVH * HD), D ** -0.5, 0.109375, ((0, 4),))
    w_output = scatter_about(key_list[8], (HEADS * HD, D), (HEADS * HD // 32) ** -0.5, 0.5, ((0, 4),))
    sink_logits = jnp.clip(2.0 + 3.0 * jax.random.uniform(key_list[9], (HEADS,), jnp.float32) ** block_levels(key_list[9], (HEADS,), ((0, 4),), -0.2, 0.2), 2.0, 5.0).astype(jnp.bfloat16)
    gain_two = jnp.clip(1.0 + 0.1 * jax.random.normal(key_list[10], (D,), jnp.float32), 0.5, 1.5).astype(jnp.bfloat16)
    w_router = scatter_about(key_list[11], (D, EXPERTS), (D // 4) ** -0.5, 0.21875, ((0, 4),))
    w_in = scatter_about(key_list[12], (EXPERTS, D, 2 * FF), (D // 6) ** -0.5, 0.25, ((0, 8), (1, 4)))
    w_out = scatter_about(key_list[13], (EXPERTS, FF, D), (16 * FF) ** -0.5, 0.02734375, ((0, 8), (1, 4)))
    return {"hidden_in": hidden_in, "out_grad": out_grad, "boundary": boundary, "routes": routes, "gain_one": gain_one, "w_query": w_query, "w_key": w_key, "w_value": w_value, "w_output": w_output, "sink_logits": sink_logits, "gain_two": gain_two, "w_router": w_router, "w_in": w_in, "w_out": w_out}


@jax.custom_vjp
def low(v):
    return lax.optimization_barrier(v.astype(jnp.bfloat16)).astype(jnp.float32)

@jax.custom_vjp
def low_back(v):
    return v

def low_keep(v):
    return (low(v), None)

def low_pass(kept, grad):
    return (grad,)

def back_keep(v):
    return (v, None)

def back_low(kept, grad):
    return (low(grad),)
low.defvjp(low_keep, low_pass)
low_back.defvjp(back_keep, back_low)
norm_eps = 1e-05
theta_base = 150000.0
limit_value = 7.0
alpha_value = 1.702
score_scale = 0.125

def matmul_high(left, right):
    return jnp.dot(left, right, precision=lax.Precision.HIGHEST)

def rms_scale(values, gain):
    return values * lax.rsqrt(lax.optimization_barrier(jnp.mean(values * values, axis=-1, keepdims=True)) + norm_eps) * gain

def rotate_half(values, cosine, sine_part):
    half_dim = values.shape[-1] // 2
    first_half = values[..., :half_dim]
    second_half = values[..., half_dim:]
    return jnp.concatenate([first_half * cosine - second_half * sine_part, second_half * cosine + first_half * sine_part], axis=-1)

def clamp_swiglu(gate, up):
    clipped = jnp.minimum(gate, limit_value)
    up_clip = jnp.clip(up, -limit_value, limit_value)
    return (up_clip + 1.0) * clipped * jax.nn.sigmoid(alpha_value * clipped)

def route_slots(route_flat, experts):
    one_hot = (route_flat[:, None] == jnp.arange(experts, dtype=jnp.int32)[None, :]).astype(jnp.int32)
    counted = jnp.cumsum(one_hot, axis=0)
    return lax.optimization_barrier(jnp.sum(one_hot * counted, axis=1)) - 1

def attend_group(query_all, key_all, value_all, sinks, split_at):
    group_len = SEQ_TOK
    block_rows = min(512, group_len)
    edge_rows = WIN - 1
    group_size = HEADS // KVH
    query_heads = query_all.reshape(group_len, KVH, group_size, HD)
    key_pad = jnp.pad(key_all.reshape(group_len, KVH, HD), ((edge_rows, 0), (0, 0), (0, 0)))
    value_pad = jnp.pad(value_all.reshape(group_len, KVH, HD), ((edge_rows, 0), (0, 0), (0, 0)))
    sink_heads = sinks.reshape(KVH, group_size)

    def one_block(block_index):
        block_start = block_index * block_rows
        query_block = lax.dynamic_slice_in_dim(query_heads, block_start, block_rows, 0)
        key_block = lax.dynamic_slice_in_dim(key_pad, block_start, block_rows + edge_rows, 0)
        value_block = lax.dynamic_slice_in_dim(value_pad, block_start, block_rows + edge_rows, 0)
        query_pos = block_start + jnp.arange(block_rows, dtype=jnp.int32)
        key_pos = block_start - edge_rows + jnp.arange(block_rows + edge_rows, dtype=jnp.int32)
        distance = query_pos[:, None] - key_pos[None, :]
        allowed = (distance >= 0) & (distance < WIN) & (key_pos[None, :] >= 0) & ((query_pos[:, None] >= split_at) == (key_pos[None, :] >= split_at))
        scores = low_back(jnp.einsum('qkgd,jkd->kgqj', query_block, key_block, precision=lax.Precision.HIGHEST) * score_scale)
        masked = jnp.where(allowed[None, None], scores, -1e+30)
        top_score = jnp.maximum(lax.optimization_barrier(jnp.max(masked, axis=3)), sink_heads[:, :, None])
        exp_scores = jnp.where(allowed[None, None], jnp.exp(masked - top_score[..., None]), 0.0)
        denom_sum = lax.optimization_barrier(jnp.sum(exp_scores, axis=3)) + jnp.exp(sink_heads[:, :, None] - top_score)
        probs_now = low(exp_scores / denom_sum[..., None])
        result = jnp.einsum('kgqj,jkd->qkgd', probs_now, value_block, precision=lax.Precision.HIGHEST)
        return result.reshape(block_rows, HEADS * HD)
    results = lax.map(jax.checkpoint(one_block), jnp.arange(group_len // block_rows, dtype=jnp.int32))
    return results.reshape(group_len, HEADS * HD)

def run_experts(h_two, routes, w_in, w_out):
    token_count = h_two.shape[0]
    blocks = token_count // TOK_DEV
    route_blocks = routes.reshape(blocks, TOK_DEV * TOP)
    slot_ids = jax.vmap(lambda row: route_slots(row, EXPERTS))(route_blocks)
    expert_ids = route_blocks.reshape(-1)
    places = (jnp.arange(blocks, dtype=jnp.int32)[:, None] * CAP + slot_ids).reshape(-1)
    routed_rows = jnp.repeat(h_two, TOP, axis=0)
    buffer = jnp.zeros((EXPERTS, blocks * CAP, D), jnp.float32).at[expert_ids, places].set(routed_rows)

    def one_expert(pieces):
        rows_now, expert_in, expert_out_w = pieces
        gate_up = low_back(matmul_high(rows_now, expert_in))
        activation = low(clamp_swiglu(gate_up[:, :FF], gate_up[:, FF:]))
        return low(low_back(matmul_high(activation, expert_out_w)))
    expert_outs = lax.map(jax.checkpoint(one_expert), (buffer, w_in, w_out))
    return expert_outs[expert_ids, places].reshape(token_count, TOP, D)

def forward_pass(hidden, gain_one, w_query, w_key, w_value, w_output, sinks, gain_two, w_router, w_in, w_out, boundary, routes):
    groups = hidden.shape[0]
    token_count = groups * SEQ_TOK
    flat_rows = hidden.reshape(token_count, D)
    h_one = low(rms_scale(flat_rows, gain_one))
    query_raw = low_back(matmul_high(h_one, w_query))
    key_raw = low_back(matmul_high(h_one, w_key))
    value_all = low(low_back(matmul_high(h_one, w_value)))
    token_pos = jnp.arange(SEQ_TOK, dtype=jnp.int32)
    segment = token_pos[None, :] >= boundary[:, None]
    positions = (token_pos[None, :] - jnp.where(segment, boundary[:, None], 0)).reshape(-1)
    half_dim = HD // 2
    frequency = jnp.exp(-jnp.log(theta_base) * (2.0 * jnp.arange(half_dim, dtype=jnp.float32)) / HD)
    angles = positions.astype(jnp.float32)[:, None] * frequency[None, :]
    cosine = jnp.cos(angles)[:, None, :]
    sine_part = jnp.sin(angles)[:, None, :]
    query_all = low(rotate_half(query_raw.reshape(token_count, HEADS, HD), cosine, sine_part))
    key_all = low(rotate_half(key_raw.reshape(token_count, KVH, HD), cosine, sine_part))
    query_all = query_all.reshape(groups, SEQ_TOK, HEADS * HD)
    key_all = key_all.reshape(groups, SEQ_TOK, KVH * HD)
    value_all = value_all.reshape(groups, SEQ_TOK, KVH * HD)
    attention = lax.map(lambda pieces: attend_group(pieces[0], pieces[1], pieces[2], sinks, pieces[3]), (query_all, key_all, value_all, boundary))
    attended = low(low_back(attention.reshape(token_count, HEADS * HD)))
    branch = low_back(matmul_high(attended, w_output))
    resid = flat_rows + branch
    h_two = low(rms_scale(resid, gain_two))
    logits = low_back(matmul_high(h_two, w_router))
    route_flat = routes.reshape(token_count, TOP)
    chosen = jnp.take_along_axis(logits, route_flat, axis=1)
    weights = jax.nn.softmax(chosen, axis=1)
    picked = run_experts(h_two, routes, w_in, w_out)
    mixture = lax.optimization_barrier(jnp.sum(weights[:, :, None] * picked, axis=1))
    return (resid + mixture).reshape(hidden.shape)

def reference(hidden_in, out_grad, boundary, routes, gain_one, w_query, w_key, w_value, w_output, sink_logits, gain_two, w_router, w_in, w_out):
    floats = (hidden_in, gain_one, w_query, w_key, w_value, w_output, sink_logits, gain_two, w_router, w_in, w_out)
    floats = tuple((item.astype(jnp.float32) for item in floats))

    def wrapped(hidden, g_one, wq, wk, wv, wo, sinks, g_two, wr, wi, wout):
        return forward_pass(hidden, g_one, wq, wk, wv, wo, sinks, g_two, wr, wi, wout, boundary, routes)
    output, pull_back = jax.vjp(wrapped, *floats)
    grad_list = pull_back(out_grad.astype(jnp.float32))
    return (output.astype(jnp.bfloat16), grad_list[0], grad_list[1], grad_list[2], grad_list[3], grad_list[4], grad_list[5], grad_list[6], grad_list[7], grad_list[8], grad_list[9], grad_list[10])
```

```python
import functools

import jax
import jax.numpy as jnp
from jax import lax
from jax.experimental import pallas as pl
from jax.experimental.layout import Layout, with_layout_constraint
from jax.experimental.pallas import tpu as pltpu
from jax.sharding import PartitionSpec as P

WIN = 128
LANES = 128

norm_eps = 1e-05
theta_base = 150000.0
limit_value = 7.0
alpha_value = 1.702
score_scale = 0.125

f32 = jnp.float32
bf16 = jnp.bfloat16


def contract_last(left, right):
    return lax.dot_general(left, right, (((1,), (1,)), ((), ())), preferred_element_type=f32)


def contract_first(left, right):
    return lax.dot_general(left, right, (((0,), (0,)), ((), ())), preferred_element_type=f32)


def matmul(left, right):
    return jnp.dot(left, right, preferred_element_type=f32)


def round_up(value, unit):
    return -(-value // unit) * unit


def partner(values):
    lane = lax.broadcasted_iota(jnp.int32, values.shape, 1)
    return jnp.where(lane % 64 < 32, pltpu.roll(values, 96, 1), pltpu.roll(values, 32, 1))


def allowed_keys(block, split_at):
    row = lax.broadcasted_iota(jnp.int32, (WIN, 2 * WIN), 0) + block * WIN
    key = lax.broadcasted_iota(jnp.int32, (WIN, 2 * WIN), 1) + (block - 1) * WIN
    distance = row - key
    return (
        (distance >= 0)
        & (distance < WIN)
        & (key >= 0)
        & ((row >= split_at) == (key >= split_at))
    )


def both_halves(keys_values, low):
    lane = lax.broadcasted_iota(jnp.int32, keys_values.shape, 1)
    other = pltpu.roll(keys_values, 64, 1)
    return jnp.where((lane < 64) == low, keys_values, other)


def attend_kernel(split_ref, sink_ref, qkv_ref, cos_ref, sin_ref, q_ref, kv_ref, att_ref, lse_ref):
    tokens = qkv_ref.shape[0]
    width = q_ref.shape[1]
    pairs = width // LANES
    split_at = split_ref[0]
    lane = lax.broadcasted_iota(jnp.int32, (WIN, LANES), 1)

    def body(block, carry):
        rows = pl.ds(pl.multiple_of(block * WIN, WIN), WIN)
        back = pl.ds(pl.multiple_of(jnp.maximum(block - 1, 0) * WIN, WIN), WIN)
        cosine = cos_ref[rows, :]
        sine = sin_ref[rows, :]
        kv_raw = qkv_ref[rows, width:]
        kv_now = jnp.where(lane < 64, kv_raw * cosine + partner(kv_raw) * sine, kv_raw)
        kv_ref[rows, :] = kv_now.astype(bf16)
        kv_two = jnp.concatenate([kv_ref[back, :].astype(f32), kv_now.astype(bf16).astype(f32)], axis=0)
        keys = both_halves(kv_two, True).astype(bf16)
        values = both_halves(kv_two, False).astype(bf16)
        allowed = allowed_keys(block, split_at)
        stats = jnp.zeros((WIN, LANES), f32)
        for pair in range(pairs):
            at = pl.ds(pair * LANES, LANES)
            raw = qkv_ref[rows, at]
            turned = (raw * cosine + partner(raw) * sine).astype(bf16)
            q_ref[rows, at] = turned
            outs = []
            for half in range(2):
                head = 2 * pair + half
                picked = jnp.where((lane < 64) == (half == 0), turned.astype(f32), 0.0).astype(bf16)
                scores = contract_last(picked, keys) * score_scale
                masked = jnp.where(allowed, scores, -1e30)
                sink = sink_ref[head]
                top = jnp.maximum(jnp.max(masked, axis=1, keepdims=True), sink)
                exps = jnp.where(allowed, jnp.exp(masked - top), 0.0)
                denom = jnp.sum(exps, axis=1, keepdims=True) + jnp.exp(sink - top)
                probs = (exps * (1.0 / denom)).astype(bf16)
                outs.append(matmul(probs, values))
                stats = jnp.where(lane == head, top + jnp.log(denom), stats)
            att_ref[rows, at] = jnp.where(lane < 64, outs[0], outs[1]).astype(bf16)
        lse_ref[rows, :] = stats
        return carry

    lax.fori_loop(0, tokens // WIN, body, 0)


def attend(split_at, sinks, qkv, cosine, sine, width):
    tokens = qkv.shape[0]
    vmem = pl.BlockSpec(memory_space=pltpu.VMEM)
    smem = pl.BlockSpec(memory_space=pltpu.SMEM)
    return pl.pallas_call(
        attend_kernel,
        out_shape=(
            jax.ShapeDtypeStruct((tokens, width), bf16),
            jax.ShapeDtypeStruct((tokens, LANES), bf16),
            jax.ShapeDtypeStruct((tokens, width), bf16),
            jax.ShapeDtypeStruct((tokens, LANES), f32),
        ),
        in_specs=[smem, smem, vmem, vmem, vmem],
        out_specs=(vmem, vmem, vmem, vmem),
        compiler_params=pltpu.CompilerParams(vmem_limit_bytes=32 * 2**20),
        cost_estimate=pl.CostEstimate(
            flops=tokens * width * 2 * WIN * 8, bytes_accessed=8 * 2**20, transcendentals=0
        ),
        name="attend",
    )(split_at, sinks, qkv, cosine, sine)


def attend_back_kernel(
    split_ref, sink_ref, q_ref, kv_ref, datt_ref, lse_ref, cos_ref, sin_ref, draw_ref, dsink_ref, dk_acc, dv_acc
):
    tokens = q_ref.shape[0]
    width = q_ref.shape[1]
    pairs = width // LANES
    split_at = split_ref[0]
    lane = lax.broadcasted_iota(jnp.int32, (WIN, LANES), 1)
    lane_row = lax.broadcasted_iota(jnp.int32, (8, LANES), 1)
    dk_acc[...] = jnp.zeros_like(dk_acc)
    dv_acc[...] = jnp.zeros_like(dv_acc)

    def body(block, sink_sum):
        rows = pl.ds(pl.multiple_of(block * WIN, WIN), WIN)
        back = pl.ds(pl.multiple_of(jnp.maximum(block - 1, 0) * WIN, WIN), WIN)
        both = pl.ds(pl.multiple_of(block * WIN, WIN), 2 * WIN)
        cosine = cos_ref[rows, :]
        sine = sin_ref[rows, :]
        kv_two = jnp.concatenate([kv_ref[back, :], kv_ref[rows, :]], axis=0).astype(f32)
        keys = both_halves(kv_two, True).astype(bf16)
        values = both_halves(kv_two, False).astype(bf16)
        allowed = allowed_keys(block, split_at)
        stats = lse_ref[rows, :]
        d_keys = jnp.zeros((2 * WIN, LANES), f32)
        d_values = jnp.zeros((2 * WIN, LANES), f32)
        for pair in range(pairs):
            at = pl.ds(pair * LANES, LANES)
            turned = q_ref[rows, at].astype(f32)
            d_out = datt_ref[rows, at].astype(f32)
            d_turned = []
            for half in range(2):
                head = 2 * pair + half
                mine = (lane < 64) == (half == 0)
                picked = jnp.where(mine, turned, 0.0).astype(bf16)
                d_picked = jnp.where(mine, d_out, 0.0).astype(bf16)
                total = stats[:, head : head + 1]
                scores = contract_last(picked, keys) * score_scale
                probs = jnp.where(allowed, jnp.exp(scores - total), 0.0)
                d_probs = contract_last(d_picked, values)
                delta = jnp.sum(probs * d_probs, axis=1, keepdims=True)
                d_scores = (probs * (d_probs - delta)).astype(bf16)
                share = jnp.sum(jnp.exp(sink_ref[head] - total) * delta)
                sink_sum = sink_sum - jnp.where(lane_row == head, share, 0.0)
                d_turned.append(matmul(d_scores, keys))
                d_keys = d_keys + contract_first(d_scores, picked)
                d_values = d_values + contract_first(probs.astype(bf16), d_picked)
            d_query = jnp.where(lane < 64, d_turned[0], d_turned[1]) * score_scale
            draw_ref[rows, at] = (d_query * cosine - partner(d_query) * sine).astype(bf16)
        dk_acc[both, :] += d_keys
        dv_acc[both, :] += d_values
        return sink_sum

    dsink_ref[...] = lax.fori_loop(0, tokens // WIN, body, jnp.zeros((8, LANES), f32))

    def finish(block, carry):
        rows = pl.ds(pl.multiple_of(block * WIN, WIN), WIN)
        held = pl.ds(pl.multiple_of((block + 1) * WIN, WIN), WIN)
        d_keys = dk_acc[held, :]
        d_keys = (d_keys + pltpu.roll(d_keys, 64, 1)) * score_scale
        d_keys = d_keys * cos_ref[rows, :] - partner(d_keys) * sin_ref[rows, :]
        d_values = dv_acc[held, :]
        d_values = d_values + pltpu.roll(d_values, 64, 1)
        draw_ref[rows, width:] = jnp.where(lane < 64, d_keys, d_values).astype(bf16)
        return carry

    lax.fori_loop(0, tokens // WIN, finish, 0)


def attend_back(split_at, sinks, queries, kv, d_att, lse, cosine, sine):
    tokens, width = queries.shape
    vmem = pl.BlockSpec(memory_space=pltpu.VMEM)
    smem = pl.BlockSpec(memory_space=pltpu.SMEM)
    return pl.pallas_call(
        attend_back_kernel,
        out_shape=(
            jax.ShapeDtypeStruct((tokens, width + LANES), bf16),
            jax.ShapeDtypeStruct((8, LANES), f32),
        ),
        in_specs=[smem, smem, vmem, vmem, vmem, vmem, vmem, vmem],
        out_specs=(vmem, vmem),
        scratch_shapes=[pltpu.VMEM((tokens + WIN, LANES), f32), pltpu.VMEM((tokens + WIN, LANES), f32)],
        compiler_params=pltpu.CompilerParams(vmem_limit_bytes=32 * 2**20),
        cost_estimate=pl.CostEstimate(
            flops=tokens * width * 2 * WIN * 20, bytes_accessed=8 * 2**20, transcendentals=0
        ),
        name="attend_back",
    )(split_at, sinks, queries, kv, d_att, lse, cosine, sine)


def expert_kernel(units, first, *refs):
    experts, capacity, tile = units
    ids_ref, h_ref, g_ref, wg_ref, wu_ref, wd_ref = refs[:6]
    refs = refs[6:] if first else refs[10:]
    back_ref, out_ref, x_ref, gr_ref, act_ref, du_ref, xf, gf = refs
    T = h_ref.shape[2]
    D = wd_ref.shape[1]
    ffp = wd_ref.shape[0]
    at_blocks = [(i, j) for i in range(h_ref.shape[0]) for j in range(h_ref.shape[1])]
    expert = ids_ref[0]
    place_col = ids_ref[1]
    tail = h_ref.shape[3] - LANES
    base = D - tail
    lane = lax.broadcasted_iota(jnp.int32, (T, LANES), 1)
    row = lax.broadcasted_iota(jnp.int32, (T, T), 0)
    col = lax.broadcasted_iota(jnp.int32, (T, T), 1)
    before = jnp.where(col < row, 1.0, 0.0).astype(bf16)
    places = []
    weights = []
    for b, (i, j) in enumerate(at_blocks):
        last = h_ref[i, j, :, tail:].astype(f32)
        hit = jnp.sum(jnp.where(lane == base + 3 * experts + expert, last, 0.0), axis=1, keepdims=True)
        hits = jnp.broadcast_to(hit, (T, LANES))
        slot = matmul(before, hits.astype(bf16))
        place = jnp.where((slot == lane.astype(f32)) & (hits > 0.5), 1.0, 0.0)[:, :capacity].astype(bf16)
        places.append(place)
        at = pl.ds(b * capacity, capacity)
        xf[at, :] = contract_first(place, h_ref[i, j])
        ends = xf[at, tail:]
        lane_c = lax.broadcasted_iota(jnp.int32, ends.shape, 1) - base - expert
        mine = (lane_c == 0) | (lane_c == experts) | (lane_c == 2 * experts)
        weight = jnp.sum(jnp.where(mine, ends, 0.0), axis=1, keepdims=True)
        weights.append(weight)
        gf[at, :] = contract_first(place, g_ref[i, j]) * weight
    x_ref[...] = xf[:, :D].astype(bf16)
    gr_ref[...] = gf[:, :D].astype(bf16)
    weight_all = jnp.concatenate(weights, axis=0)
    share = jnp.zeros_like(weight_all)
    for n in range(ffp // tile):
        at = pl.ds(n * tile, tile)
        at_up = pl.ds(ffp + n * tile, tile)
        gate = matmul(x_ref[...], wg_ref[:, at])
        up = matmul(x_ref[...], wu_ref[:, at])
        d_act = contract_last(gr_ref[...], wd_ref[at, :])
        clipped = jnp.minimum(gate, limit_value)
        up_one = jnp.clip(up, -limit_value, limit_value) + 1.0
        sig = 1.0 / (1.0 + jnp.exp(-alpha_value * clipped))
        swish = clipped * sig
        act = (up_one * swish).astype(bf16)
        act_ref[:, at] = act
        share = share + jnp.sum(act.astype(f32) * d_act, axis=1, keepdims=True)
        d_gate = jnp.where(
            gate < limit_value, d_act * up_one * (sig + alpha_value * swish * (1.0 - sig)), 0.0
        )
        d_up = jnp.where((up > -limit_value) & (up < limit_value), d_act * swish, 0.0)
        du_ref[:, at] = d_gate.astype(bf16)
        du_ref[:, at_up] = d_up.astype(bf16)
    step = 768
    for start in range(0, D, step):
        size = min(step, D - start)
        d_rows = contract_last(du_ref[:, :ffp], wg_ref[start : start + size, :])
        d_rows = d_rows + contract_last(du_ref[:, ffp:], wu_ref[start : start + size, :])
        for b, (i, j) in enumerate(at_blocks):
            part = d_rows[b * capacity : (b + 1) * capacity].astype(bf16)
            back_ref[i, j, :, start : start + size] = matmul(places[b], part).astype(bf16)
    high = share.astype(bf16).astype(f32)
    spare = back_ref.shape[3] - D
    lane_s = lax.broadcasted_iota(jnp.int32, (capacity, spare), 1)
    for b, (i, j) in enumerate(at_blocks):
        own = slice(b * capacity, (b + 1) * capacity)
        terms = jnp.where(lane_s == place_col, high[own], 0.0)
        terms = jnp.where(lane_s == place_col + 1, share[own] - high[own], terms)
        back_ref[i, j, :, D:] = matmul(places[b], terms.astype(bf16)).astype(bf16)
    for start in range(0, D, step):
        size = min(step, D - start)
        rows = matmul(act_ref[...], wd_ref[:, start : start + size]) * weight_all
        for b, (i, j) in enumerate(at_blocks):
            part = rows[b * capacity : (b + 1) * capacity].astype(bf16)
            out_ref[i, j, :, start : start + size] = matmul(places[b], part).astype(bf16)


def run_expert(ids, h_part, g_all, w_gate, w_up, w_down, experts, capacity, spare, half, kept):
    S, FH, T, wide = h_part.shape
    ffp, D = w_down.shape
    lead = max(1, 4 // FH)
    steps = S // lead
    tile = 256 if ffp % 256 == 0 else LANES
    rows = lead * FH * capacity
    smem = pl.BlockSpec(memory_space=pltpu.SMEM)
    held = pl.BlockSpec(memory_space=pl.ANY)

    def tokens(width):
        return pl.BlockSpec((lead, FH, T, width), lambda i: (i, 0, 0, 0))

    def slots(width):
        return pl.BlockSpec((rows, width), lambda i: (i + half * steps, 0))

    def whole(shape):
        return pl.BlockSpec(shape, lambda i: (0, 0), pipeline_mode=pl.Buffered(1))

    total = 2 * S * FH * capacity
    first = kept is None
    extra = () if first else tuple(kept)
    return pl.pallas_call(
        functools.partial(expert_kernel, (experts, capacity, tile), first),
        grid=(steps,),
        out_shape=(
            jax.ShapeDtypeStruct((S, FH, T, D + spare), bf16),
            jax.ShapeDtypeStruct((S, FH, T, D), bf16),
            jax.ShapeDtypeStruct((total, D), bf16),
            jax.ShapeDtypeStruct((total, D), bf16),
            jax.ShapeDtypeStruct((total, ffp), bf16),
            jax.ShapeDtypeStruct((total, 2 * ffp), bf16),
        ),
        in_specs=[smem, tokens(wide), pl.BlockSpec((lead, FH, T, wide), lambda i: (i, half, 0, 0))]
        + [whole(w.shape) for w in (w_gate, w_up, w_down)]
        + [held] * len(extra),
        out_specs=(
            tokens(D + spare), tokens(D), slots(D), slots(D), slots(ffp), slots(2 * ffp),
        ),
        input_output_aliases={6 + k: 2 + k for k in range(len(extra))},
        scratch_shapes=[pltpu.VMEM((rows, wide), f32)] * 2,
        compiler_params=pltpu.CompilerParams(vmem_limit_bytes=62 * 2**20),
        cost_estimate=pl.CostEstimate(
            flops=total * D * ffp * 6, bytes_accessed=60 * 2**20, transcendentals=0
        ),
        name="experts",
    )(ids, h_part, g_all, w_gate, w_up, w_down, *extra)


def rows_at_once(rows):
    return 144 if rows % 144 == 0 else rows


def cut_kernel(parts, ff, w_ref, gate_ref, up_ref):
    for half, out_ref in enumerate((gate_ref, up_ref)):
        ffp = out_ref.shape[2]
        for part in range(parts):
            first = (half * parts + part) * ff
            out_ref[part, :, :ff] = w_ref[:, first : first + ff]
            if ffp > ff:
                out_ref[part, :, ff:] = jnp.zeros((w_ref.shape[0], ffp - ff), bf16)


def cut_units(w, parts, ff, ffp):
    rows = w.shape[0]
    step = rows_at_once(rows)
    return pl.pallas_call(
        functools.partial(cut_kernel, parts, ff),
        grid=(rows // step,),
        out_shape=(jax.ShapeDtypeStruct((parts, rows, ffp), bf16),) * 2,
        in_specs=[pl.BlockSpec((step, w.shape[1]), lambda i: (i, 0))],
        out_specs=(pl.BlockSpec((parts, step, ffp), lambda i: (0, i, 0)),) * 2,
        compiler_params=pltpu.CompilerParams(vmem_limit_bytes=40 * 2**20),
        cost_estimate=pl.CostEstimate(flops=0, bytes_accessed=4 * w.size, transcendentals=0),
        name="cut_units",
    )(w)


def join_kernel(ff, gate_ref, up_ref, out_ref):
    for half, g_ref in enumerate((gate_ref, up_ref)):
        parts = g_ref.shape[0]
        for part in range(parts):
            first = (half * parts + part) * ff
            out_ref[:, first : first + ff] = g_ref[part, :, :ff].astype(f32)


def join_units(gate, up, ff):
    parts, rows, width = gate.shape
    step = rows_at_once(rows)
    return pl.pallas_call(
        functools.partial(join_kernel, ff),
        grid=(rows // step,),
        out_shape=jax.ShapeDtypeStruct((rows, 2 * parts * ff), f32),
        in_specs=[pl.BlockSpec((parts, step, width), lambda i: (0, i, 0))] * 2,
        out_specs=pl.BlockSpec((step, 2 * parts * ff), lambda i: (i, 0)),
        compiler_params=pltpu.CompilerParams(vmem_limit_bytes=48 * 2**20),
        cost_estimate=pl.CostEstimate(flops=0, bytes_accessed=12 * gate.size, transcendentals=0),
        name="join_units",
    )(gate, up)


def heads_kernel(q_cols, head_dim, g_ref, q_ref, k_ref, v_ref):
    sources = g_ref.shape[0]
    kv_heads = k_ref.shape[1] // head_dim
    repeat = sources // kv_heads
    for source in range(sources):
        q_ref[:, source * q_cols : (source + 1) * q_cols] = g_ref[source, :, :q_cols].astype(f32)
    for out_ref, begin in ((k_ref, q_cols), (v_ref, q_cols + head_dim)):
        for head in range(kv_heads):
            total = g_ref[head * repeat, :, begin : begin + head_dim].astype(f32)
            for other in range(1, repeat):
                total = total + g_ref[head * repeat + other, :, begin : begin + head_dim].astype(f32)
            out_ref[:, head * head_dim : (head + 1) * head_dim] = total


def join_heads(grads, q_cols, head_dim, kv_heads):
    sources, rows, width = grads.shape
    step = rows_at_once(rows)
    kv_cols = kv_heads * head_dim
    return pl.pallas_call(
        functools.partial(heads_kernel, q_cols, head_dim),
        grid=(rows // step,),
        out_shape=(
            jax.ShapeDtypeStruct((rows, sources * q_cols), f32),
            jax.ShapeDtypeStruct((rows, kv_cols), f32),
            jax.ShapeDtypeStruct((rows, kv_cols), f32),
        ),
        in_specs=[pl.BlockSpec((sources, step, width), lambda i: (0, i, 0))],
        out_specs=(
            pl.BlockSpec((step, sources * q_cols), lambda i: (i, 0)),
            pl.BlockSpec((step, kv_cols), lambda i: (i, 0)),
            pl.BlockSpec((step, kv_cols), lambda i: (i, 0)),
        ),
        compiler_params=pltpu.CompilerParams(vmem_limit_bytes=48 * 2**20),
        cost_estimate=pl.CostEstimate(flops=0, bytes_accessed=6 * grads.size, transcendentals=0),
        name="join_heads",
    )(grads)


def gather_direct(value, axis):
    count = lax.axis_size(axis)
    spread = jnp.broadcast_to(value[None], (count,) + value.shape)
    return lax.all_to_all(spread, axis, split_axis=0, concat_axis=0, tiled=True)


def sum_direct(parts, axis):
    got = lax.all_to_all(parts, axis, split_axis=0, concat_axis=0, tiled=True)
    return jnp.sum(got.astype(f32), axis=0)


def shifted(value, axis, steps):
    count = lax.axis_size(axis)
    return lax.ppermute(value, axis, [(i, (i + steps) % count) for i in range(count)])


def taken(parts, index):
    return lax.dynamic_index_in_dim(parts, index, 0, keepdims=False)


def sent(parts, k):
    count = lax.axis_size("fsdp")
    return shifted(taken(parts, (lax.axis_index("fsdp") + k) % count), "fsdp", k)


def placed_parts(parts, got):
    count = lax.axis_size("fsdp")
    for k, piece in got.items():
        parts = lax.dynamic_update_index_in_dim(
            parts, piece, (lax.axis_index("fsdp") - k) % count, 0
        )
    return parts


def summed_parts(parts, got):
    total = taken(parts, lax.axis_index("fsdp")).astype(f32)
    for piece in got:
        total = total + piece.astype(f32)
    return total


def sum_turned(parts, axis):
    total = parts[0].astype(f32)
    for k in range(1, len(parts)):
        total = total + shifted(parts[k], axis, -k).astype(f32)
    return total


def row_major(value):
    return with_layout_constraint(value, Layout(major_to_minor=tuple(range(value.ndim))))


def after(value, *others):
    return lax.optimization_barrier((value,) + others)[0]


def together(*lists):
    flat = lax.optimization_barrier(tuple(item for items in lists for item in items))
    result, at = [], 0
    for items in lists:
        result.append(list(flat[at : at + len(items)]))
        at += len(items)
    return result


def flat_tiles(items, dtype):
    flat = jnp.concatenate([item.reshape(-1) for item in items]).astype(dtype)
    padded = round_up(flat.shape[0], 16 * LANES)
    return jnp.pad(flat, (0, padded - flat.shape[0])).reshape(-1, LANES)


def back_kernel(d_ref, w_ref, x_ref, r_ref, out_ref, gain_ref):
    d_h = contract_last(d_ref[...], w_ref[...])
    out_ref[...] = d_h.astype(bf16)
    sums = jnp.sum(d_h * x_ref[...].astype(f32) * r_ref[...], axis=0, keepdims=True)

    @pl.when(pl.program_id(0) == 0)
    def _():
        gain_ref[...] = jnp.zeros_like(gain_ref)

    gain_ref[...] += jnp.broadcast_to(sums, gain_ref.shape)


def rows_back(d_raw, w_qkv, x_all, r_all):
    rows, width = d_raw.shape
    D = w_qkv.shape[0]
    step = 256
    return pl.pallas_call(
        back_kernel,
        grid=(rows // step,),
        out_shape=(jax.ShapeDtypeStruct((rows, D), bf16), jax.ShapeDtypeStruct((8, D), f32)),
        in_specs=[
            pl.BlockSpec((step, width), lambda i: (i, 0)),
            pl.BlockSpec((D, width), lambda i: (0, 0)),
            pl.BlockSpec((step, D), lambda i: (i, 0)),
            pl.BlockSpec((step, 1), lambda i: (i, 0)),
        ],
        out_specs=(pl.BlockSpec((step, D), lambda i: (i, 0)), pl.BlockSpec((8, D), lambda i: (0, 0))),
        compiler_params=pltpu.CompilerParams(vmem_limit_bytes=40 * 2**20),
        cost_estimate=pl.CostEstimate(
            flops=2 * rows * D * width, bytes_accessed=20 * 2**20, transcendentals=0
        ),
        name="rows_back",
    )(d_raw, w_qkv, x_all, r_all)


def spread_tables(S, F):
    ratio = S // F
    return [[(src, ((src + k) % F) * ratio + src // F) for src in range(S)] for k in range(F)]


def gather_heads(pieces, s, S, F):
    ratio = S // F
    rows = jnp.zeros_like(pieces)
    for k, perm in enumerate(spread_tables(S, F)):
        sent = lax.dynamic_index_in_dim(pieces, (s + k) % F, 0, keepdims=False)
        got = lax.ppermute(sent, "seq", perm)
        rows = lax.dynamic_update_index_in_dim(rows, got, (s // ratio - k) % F, 0)
    return rows


def return_heads(rows, s, S, F):
    ratio = S // F
    got = []
    for k, perm in enumerate(spread_tables(S, F)):
        sent = lax.dynamic_index_in_dim(rows, (s // ratio - k) % F, 0, keepdims=False)
        got.append(lax.ppermute(sent, "seq", [(b, a) for a, b in perm]))
    return got


def return_places(got, s):
    pieces = jnp.broadcast_to(got[0][None], (len(got),) + got[0].shape)
    for k, piece in enumerate(got):
        pieces = lax.dynamic_update_index_in_dim(pieces, piece, (s + k) % len(got), 0)
    return pieces


def local(
    hidden_in,
    out_grad,
    boundary,
    routes,
    gain_one,
    w_query,
    w_key,
    w_value,
    w_output,
    sink_logits,
    gain_two,
    w_router,
    w_in,
    w_out,
):
    S = lax.axis_size("seq")
    F = lax.axis_size("fsdp")
    s = lax.axis_index("seq")
    z = lax.axis_index("fsdp")
    T, D = hidden_in.shape[1:]
    Tg = S * T
    rows_d = w_query.shape[0]
    heads = sink_logits.shape[0] * F
    head_dim = w_query.shape[1] // heads
    kv_heads = w_key.shape[1] // head_dim
    group_size = heads // kv_heads
    heads_own = heads // S
    q_cols = heads_own * head_dim
    experts = w_router.shape[1]
    top_count = routes.shape[2]
    capacity = T * top_count * 9 // (8 * experts)
    ff = w_out.shape[1]
    ffp = round_up(ff, LANES)
    sub = w_output.shape[0] // S
    ratio = S // F

    x_own = hidden_in[0]
    x_all = row_major(lax.all_gather(row_major(x_own), "seq", axis=0, tiled=True))

    kv_head = (s * heads_own) // group_size
    qkv_shard = jnp.concatenate(
        [
            lax.dynamic_slice_in_dim(w_query, s * q_cols, q_cols, 1),
            lax.dynamic_slice_in_dim(w_key, kv_head * head_dim, head_dim, 1),
            lax.dynamic_slice_in_dim(w_value, kv_head * head_dim, head_dim, 1),
        ],
        axis=1,
    )
    w_qkv = lax.all_gather(after(qkv_shard, x_all), "fsdp", axis=0, tiled=True)

    small = flat_tiles((gain_one, gain_two, sink_logits, w_router), bf16)
    small_all = gather_direct(small, "fsdp").reshape(F, -1)
    own_sinks = sink_logits.shape[0]
    cut = [rows_d, 2 * rows_d, 2 * rows_d + own_sinks, 2 * rows_d + own_sinks + rows_d * experts]
    g_one = small_all[:, : cut[0]].reshape(1, D).astype(f32)
    g_two = small_all[:, cut[0] : cut[1]].reshape(1, D).astype(f32)
    sink_all = small_all[:, cut[1] : cut[2]].reshape(heads).astype(f32)
    wr_all = small_all[:, cut[2] : cut[3]].reshape(D, experts)
    sinks = lax.dynamic_slice_in_dim(sink_all, s * heads_own, heads_own, 0)

    split_at = boundary[0]
    token = jnp.arange(Tg, dtype=jnp.int32)
    positions = token - jnp.where(token >= split_at, split_at, 0)
    half_dim = head_dim // 2
    frequency = jnp.exp(-jnp.log(theta_base) * (2.0 * jnp.arange(half_dim, dtype=f32)) / head_dim)
    angles = positions.astype(f32)[:, None] * frequency[None, :]
    cos_half, sin_half = jnp.cos(angles), jnp.sin(angles)
    cosine = jnp.concatenate([cos_half] * 4, axis=1)
    sine = jnp.concatenate([-sin_half, sin_half] * 2, axis=1)

    x_all_f = x_all.astype(f32)
    r_one_all = lax.rsqrt(jnp.mean(x_all_f * x_all_f, axis=1, keepdims=True) + norm_eps)
    h_one = (x_all_f * r_one_all * g_one).astype(bf16)
    wo_sub = lax.dynamic_slice_in_dim(w_output, s * sub, sub, 0)
    wo_pieces = jnp.broadcast_to(wo_sub[None], (F, sub, D))
    for k in range(1, F):
        wo_pieces = lax.dynamic_update_index_in_dim(
            wo_pieces, shifted(wo_sub, "fsdp", k), (z - k) % F, 0
        )
    wo_own = gather_heads(wo_pieces, s, S, F).reshape(F * sub, D)

    half = F // 2
    wide = round_up(D + 4 * experts, LANES)
    near = [1, F - 1]
    far = [k for k in range(1, F) if k not in near]
    d_own = jnp.pad(out_grad[0], ((0, 0), (0, wide - D)))
    cut_gate, cut_up = cut_units(w_in[0], F, ff, ffp)
    w_down = jnp.pad(w_out[0], ((0, ffp - ff), (0, 0)))
    d_own, cut_gate, cut_up, w_down, w_qkv = lax.optimization_barrier(
        (d_own, cut_gate, cut_up, w_down, w_qkv)
    )
    qkv = matmul(h_one, w_qkv)
    queries, kv, attended, lse = attend(boundary, sinks, qkv, cosine, sine, q_cols)
    d_out_got = [shifted(d_own, "fsdp", k) for k in range(1, F)]
    gate_near = [sent(cut_gate, k) for k in near]

    branch_part = row_major(matmul(attended, wo_own).astype(bf16))
    branch = lax.psum_scatter(branch_part, "seq", scatter_dimension=0, tiled=True)
    (branch,), d_out_got, gate_near = together([branch], d_out_got, gate_near)

    def over_seq(pieces, *others):
        return row_major(lax.all_gather(after(row_major(jnp.stack(pieces)), *others), "seq", axis=0))

    d_out_all = over_seq([d_own] + d_out_got)
    x_f = x_own.astype(f32)
    resid = x_f + branch.astype(f32)
    r_two = lax.rsqrt(jnp.mean(resid * resid, axis=1, keepdims=True) + norm_eps)
    h_two = (resid * r_two * g_two).astype(bf16)

    blocks = S * F
    one_hot = (routes[0][:, :, None] == jnp.arange(experts, dtype=jnp.int32)).astype(f32)
    logits = matmul(h_two, wr_all)
    chosen = jnp.sum(one_hot * logits[:, None, :], axis=2)
    weights = jax.nn.softmax(chosen, axis=1)
    weight_e = jnp.sum(one_hot * weights[:, :, None], axis=1)
    hit_e = jnp.sum(one_hot, axis=1)
    high = lax.reduce_precision(weight_e, 8, 7)
    middle = lax.reduce_precision(weight_e - high, 8, 7)
    low = weight_e - high - middle
    fill = jnp.zeros((T, wide - D - 4 * experts), bf16)
    h_two_wide = jnp.concatenate(
        [h_two] + [part.astype(bf16) for part in (high, middle, low, hit_e)] + [fill], axis=1
    )

    h_two_got = [shifted(h_two_wide, "fsdp", k) for k in range(1, F)]
    h_two_got, (cut_gate, cut_up) = together(h_two_got, [cut_gate, cut_up])
    h_turned = [h_two_wide] + h_two_got
    h_parts = [over_seq(h_turned[:half])]
    h_parts.append(over_seq(h_turned[half:], h_parts[0]))
    gate_far = [sent(cut_gate, k) for k in far]
    up_got = [sent(cut_up, k) for k in range(1, F)]
    (h_parts[0],), gate_far, up_got = together(h_parts[:1], gate_far, up_got)
    w_gate = placed_parts(cut_gate, dict(zip(near + far, gate_near + gate_far))).reshape(D, ffp)
    w_up = placed_parts(cut_up, dict(zip(range(1, F), up_got))).reshape(D, ffp)

    spare = round_up(D + 2 * experts * F, LANES) - D
    ids = jnp.stack([s, 2 * (s * F + z)])
    kept = None
    backs, outs = [], []

    def to_group(parts, *others):
        got = lax.psum_scatter(after(parts, *others), "seq", scatter_dimension=0, tiled=True)
        return row_major(got)[0]

    for at in range(2):
        back, out_part, *kept = run_expert(
            ids, h_parts[at], d_out_all, w_gate, w_up, w_down, experts, capacity, spare, at, kept
        )
        backs.append(to_group(back))
        outs.append(out_part)
    rows_x, rows_g, activation, d_units = kept

    grad_gate = row_major(contract_first(rows_x, d_units[:, :ffp]).astype(bf16)).reshape(F, rows_d, ffp)
    grad_up = row_major(contract_first(rows_x, d_units[:, ffp:]).astype(bf16)).reshape(F, rows_d, ffp)
    grad_down = contract_first(activation, rows_g)[:ff]
    gate_back = {1: sent(grad_gate, 1)}
    (backs[1], gate_back[1]), (grad_gate, grad_up, grad_down) = together(
        [backs[1], gate_back[1]], [grad_gate, grad_up, grad_down]
    )
    d_wide = sum_turned([part[k] for part in backs for k in range(half)], "fsdp")
    d_wide, grad_gate, grad_up = lax.optimization_barrier((d_wide, grad_gate, grad_up))

    d_h_two = d_wide[:, :D]
    share_e = d_wide[:, D : D + 2 * experts * F].reshape(T, experts, 2 * F).sum(axis=2)
    shares = jnp.sum(one_hot * share_e[:, None, :], axis=2)
    d_chosen = shares - weights * jnp.sum(shares, axis=1, keepdims=True)
    d_logits = jnp.sum(one_hot * d_chosen[:, :, None], axis=1).astype(bf16)
    d_h_two = d_h_two + contract_last(d_logits, wr_all)
    grad_router = contract_first(h_two, d_logits)

    d_out = out_grad[0].astype(f32)
    scaled_two = g_two * d_h_two
    d_resid = (
        d_out
        + r_two * scaled_two
        - resid * (r_two * r_two * r_two) * jnp.mean(resid * scaled_two, axis=1, keepdims=True)
    )
    grad_gain_two = jnp.sum(d_h_two * resid * r_two, axis=0)

    mix_first = to_group(outs[0], backs[1])
    d_branch = row_major(lax.all_gather(row_major(d_resid.astype(bf16)), "seq", axis=0, tiled=True))
    up_back = {}
    if F > 2:
        gate_back[F - 1] = sent(grad_gate, F - 1)
        up_back[1] = sent(grad_up, 1)
        (d_branch, gate_back[F - 1], up_back[1]), (grad_gate, grad_up) = together(
            [d_branch, gate_back[F - 1], up_back[1]], [grad_gate, grad_up]
        )
    d_att = contract_last(d_branch, wo_own).astype(bf16)
    grad_wo = contract_first(after(attended, d_att), d_branch).astype(bf16).reshape(F, sub, D)
    grad_wo = return_heads(row_major(grad_wo), s, S, F)
    d_raw, d_sinks = attend_back(boundary, sinks, queries, kv, d_att, lse, cosine, sine)
    d_h_part, grad_gain_one = rows_back(d_raw, w_qkv, x_all, r_one_all)
    d_h_one = lax.psum_scatter(d_h_part, "seq", scatter_dimension=0, tiled=True).astype(f32)
    grad_gain_one = grad_gain_one[0]
    mix_second = to_group(outs[1], d_h_part)
    r_one = lax.rsqrt(jnp.mean(x_f * x_f, axis=1, keepdims=True) + norm_eps)
    scaled_one = g_one * d_h_one
    input_grad = (
        d_resid
        + r_one * scaled_one
        - x_f * (r_one * r_one * r_one) * jnp.mean(x_f * scaled_one, axis=1, keepdims=True)
    )

    grad_qkv = contract_first(after(h_one, d_h_part), d_raw).astype(bf16)
    grad_qkv = row_major(grad_qkv).reshape(F, rows_d, q_cols + 2 * head_dim)
    rest = [k for k in range(1, F) if k not in gate_back]
    gate_rest = [sent(grad_gate, k) for k in rest]
    (grad_qkv,), grad_wo, gate_rest = together([grad_qkv], grad_wo, gate_rest)
    gate_back.update(zip(rest, gate_rest))
    grad_wo = return_places(grad_wo, s)
    qkv_got = [sent(grad_qkv, k) for k in range(1, F)]
    wo_got = [sent(grad_wo, k) for k in range(1, F)]
    qkv_got, wo_got, (grad_up,) = together(qkv_got, wo_got, [grad_up])
    grad_qkv = summed_parts(grad_qkv, qkv_got).astype(bf16)
    grad_wo = summed_parts(grad_wo, wo_got).astype(bf16)
    grad_qkv = lax.all_gather(grad_qkv, "seq", axis=0)
    grad_output = row_major(lax.all_gather(row_major(grad_wo), "seq", axis=0, tiled=True)).astype(f32)
    grad_query, grad_key, grad_value = join_heads(grad_qkv, q_cols, head_dim, kv_heads)

    for k in range(1, F):
        if k not in up_back:
            up_back[k] = sent(grad_up, k)
    grad_expert_in = join_units(placed_parts(grad_gate, gate_back), placed_parts(grad_up, up_back), ff)[None]

    mixture = sum_turned([part[k] for part in (mix_first, mix_second) for k in range(half)], "fsdp")
    block_out = (resid + mixture).astype(bf16)

    own_heads = jnp.zeros((heads,), f32)
    own_heads = lax.dynamic_update_slice_in_dim(own_heads, d_sinks[0, :heads_own], s * heads_own, 0)
    tiny = jnp.concatenate(
        [
            grad_gain_one.reshape(F, rows_d),
            grad_gain_two.reshape(F, rows_d),
            own_heads.reshape(F, own_sinks),
            grad_router.reshape(F, rows_d * experts),
        ],
        axis=1,
    )
    tiny = jnp.pad(tiny, ((0, 0), (0, round_up(cut[3], 16 * LANES) - cut[3]))).reshape(F, -1, LANES)
    tiny = jnp.sum(gather_direct(sum_direct(tiny, "fsdp"), "seq"), axis=0).reshape(-1)

    return (
        block_out[None],
        input_grad[None],
        tiny[: cut[0]],
        grad_query,
        grad_key,
        grad_value,
        grad_output,
        tiny[cut[1] : cut[2]],
        tiny[cut[0] : cut[1]],
        tiny[cut[2] : cut[3]].reshape(rows_d, experts),
        grad_expert_in,
        grad_down[None],
    )


def solution(mesh):
    tokens = P("fsdp", "seq", None)
    vector = P("fsdp")
    matrix = P("fsdp", None)
    expert = P("seq", "fsdp", None)
    return jax.shard_map(
        local,
        mesh=mesh,
        in_specs=(
            tokens, tokens, vector, tokens, vector, matrix, matrix, matrix, matrix, vector, vector, matrix, expert, expert,
        ),
        out_specs=(
            tokens, tokens, vector, matrix, matrix, matrix, matrix, vector, vector, matrix, expert, expert,
        ),
        check_vma=False,
    )
```

```python
import functools

import jax
import jax.numpy as jnp
from jax import lax
from jax.experimental import pallas as pl
from jax.experimental.layout import Layout, with_layout_constraint
from jax.experimental.pallas import tpu as pltpu
from jax.sharding import PartitionSpec as P

WIN = 128
LANES = 128

norm_eps = 1e-05
theta_base = 150000.0
limit_value = 7.0
alpha_value = 1.702
score_scale = 0.125

f32 = jnp.float32
bf16 = jnp.bfloat16


def contract_last(left, right):
    return lax.dot_general(left, right, (((1,), (1,)), ((), ())), preferred_element_type=f32)


def contract_first(left, right):
    return lax.dot_general(left, right, (((0,), (0,)), ((), ())), preferred_element_type=f32)


def matmul(left, right):
    return jnp.dot(left, right, preferred_element_type=f32)


def round_up(value, unit):
    return -(-value // unit) * unit


def partner(values):
    lane = lax.broadcasted_iota(jnp.int32, values.shape, 1)
    return jnp.where(lane % 64 < 32, pltpu.roll(values, 96, 1), pltpu.roll(values, 32, 1))


def allowed_keys(block, split_at):
    row = lax.broadcasted_iota(jnp.int32, (WIN, 2 * WIN), 0) + block * WIN
    key = lax.broadcasted_iota(jnp.int32, (WIN, 2 * WIN), 1) + (block - 1) * WIN
    distance = row - key
    return (
        (distance >= 0)
        & (distance < WIN)
        & (key >= 0)
        & ((row >= split_at) == (key >= split_at))
    )


def both_halves(keys_values, low):
    lane = lax.broadcasted_iota(jnp.int32, keys_values.shape, 1)
    other = pltpu.roll(keys_values, 64, 1)
    return jnp.where((lane < 64) == low, keys_values, other)


def attend_kernel(split_ref, sink_ref, qkv_ref, cos_ref, sin_ref, q_ref, kv_ref, att_ref, lse_ref):
    tokens = qkv_ref.shape[0]
    width = q_ref.shape[1]
    pairs = width // LANES
    split_at = split_ref[0]
    lane = lax.broadcasted_iota(jnp.int32, (WIN, LANES), 1)

    def body(block, carry):
        rows = pl.ds(pl.multiple_of(block * WIN, WIN), WIN)
        back = pl.ds(pl.multiple_of(jnp.maximum(block - 1, 0) * WIN, WIN), WIN)
        cosine = cos_ref[rows, :]
        sine = sin_ref[rows, :]
        kv_raw = qkv_ref[rows, width:]
        kv_now = jnp.where(lane < 64, kv_raw * cosine + partner(kv_raw) * sine, kv_raw)
        kv_ref[rows, :] = kv_now.astype(bf16)
        kv_two = jnp.concatenate([kv_ref[back, :].astype(f32), kv_now.astype(bf16).astype(f32)], axis=0)
        keys = both_halves(kv_two, True).astype(bf16)
        values = both_halves(kv_two, False).astype(bf16)
        allowed = allowed_keys(block, split_at)
        stats = jnp.zeros((WIN, LANES), f32)
        for pair in range(pairs):
            at = pl.ds(pair * LANES, LANES)
            raw = qkv_ref[rows, at]
            turned = (raw * cosine + partner(raw) * sine).astype(bf16)
            q_ref[rows, at] = turned
            outs = []
            for half in range(2):
                head = 2 * pair + half
                picked = jnp.where((lane < 64) == (half == 0), turned.astype(f32), 0.0).astype(bf16)
                scores = contract_last(picked, keys) * score_scale
                masked = jnp.where(allowed, scores, -1e30)
                sink = sink_ref[head]
                top = jnp.maximum(jnp.max(masked, axis=1, keepdims=True), sink)
                exps = jnp.where(allowed, jnp.exp(masked - top), 0.0)
                denom = jnp.sum(exps, axis=1, keepdims=True) + jnp.exp(sink - top)
                probs = (exps * (1.0 / denom)).astype(bf16)
                outs.append(matmul(probs, values))
                stats = jnp.where(lane == head, top + jnp.log(denom), stats)
            att_ref[rows, at] = jnp.where(lane < 64, outs[0], outs[1]).astype(bf16)
        lse_ref[rows, :] = stats
        return carry

    lax.fori_loop(0, tokens // WIN, body, 0)


def attend(split_at, sinks, qkv, cosine, sine, width):
    tokens = qkv.shape[0]
    vmem = pl.BlockSpec(memory_space=pltpu.VMEM)
    smem = pl.BlockSpec(memory_space=pltpu.SMEM)
    return pl.pallas_call(
        attend_kernel,
        out_shape=(
            jax.ShapeDtypeStruct((tokens, width), bf16),
            jax.ShapeDtypeStruct((tokens, LANES), bf16),
            jax.ShapeDtypeStruct((tokens, width), bf16),
            jax.ShapeDtypeStruct((tokens, LANES), f32),
        ),
        in_specs=[smem, smem, vmem, vmem, vmem],
        out_specs=(vmem, vmem, vmem, vmem),
        compiler_params=pltpu.CompilerParams(vmem_limit_bytes=32 * 2**20),
        cost_estimate=pl.CostEstimate(
            flops=tokens * width * 2 * WIN * 8, bytes_accessed=8 * 2**20, transcendentals=0
        ),
        name="attend",
    )(split_at, sinks, qkv, cosine, sine)


def attend_back_kernel(
    split_ref, sink_ref, q_ref, kv_ref, datt_ref, lse_ref, cos_ref, sin_ref, draw_ref, dsink_ref, dk_acc, dv_acc
):
    tokens = q_ref.shape[0]
    width = q_ref.shape[1]
    pairs = width // LANES
    split_at = split_ref[0]
    lane = lax.broadcasted_iota(jnp.int32, (WIN, LANES), 1)
    lane_row = lax.broadcasted_iota(jnp.int32, (8, LANES), 1)
    dk_acc[...] = jnp.zeros_like(dk_acc)
    dv_acc[...] = jnp.zeros_like(dv_acc)

    def body(block, sink_sum):
        rows = pl.ds(pl.multiple_of(block * WIN, WIN), WIN)
        back = pl.ds(pl.multiple_of(jnp.maximum(block - 1, 0) * WIN, WIN), WIN)
        both = pl.ds(pl.multiple_of(block * WIN, WIN), 2 * WIN)
        cosine = cos_ref[rows, :]
        sine = sin_ref[rows, :]
        kv_two = jnp.concatenate([kv_ref[back, :], kv_ref[rows, :]], axis=0).astype(f32)
        keys = both_halves(kv_two, True).astype(bf16)
        values = both_halves(kv_two, False).astype(bf16)
        allowed = allowed_keys(block, split_at)
        stats = lse_ref[rows, :]
        d_keys = jnp.zeros((2 * WIN, LANES), f32)
        d_values = jnp.zeros((2 * WIN, LANES), f32)
        for pair in range(pairs):
            at = pl.ds(pair * LANES, LANES)
            turned = q_ref[rows, at].astype(f32)
            d_out = datt_ref[rows, at].astype(f32)
            d_turned = []
            for half in range(2):
                head = 2 * pair + half
                mine = (lane < 64) == (half == 0)
                picked = jnp.where(mine, turned, 0.0).astype(bf16)
                d_picked = jnp.where(mine, d_out, 0.0).astype(bf16)
                total = stats[:, head : head + 1]
                scores = contract_last(picked, keys) * score_scale
                probs = jnp.where(allowed, jnp.exp(scores - total), 0.0)
                d_probs = contract_last(d_picked, values)
                delta = jnp.sum(probs * d_probs, axis=1, keepdims=True)
                d_scores = (probs * (d_probs - delta)).astype(bf16)
                share = jnp.sum(jnp.exp(sink_ref[head] - total) * delta)
                sink_sum = sink_sum - jnp.where(lane_row == head, share, 0.0)
                d_turned.append(matmul(d_scores, keys))
                d_keys = d_keys + contract_first(d_scores, picked)
                d_values = d_values + contract_first(probs.astype(bf16), d_picked)
            d_query = jnp.where(lane < 64, d_turned[0], d_turned[1]) * score_scale
            draw_ref[rows, at] = (d_query * cosine - partner(d_query) * sine).astype(bf16)
        dk_acc[both, :] += d_keys
        dv_acc[both, :] += d_values
        return sink_sum

    dsink_ref[...] = lax.fori_loop(0, tokens // WIN, body, jnp.zeros((8, LANES), f32))

    def finish(block, carry):
        rows = pl.ds(pl.multiple_of(block * WIN, WIN), WIN)
        held = pl.ds(pl.multiple_of((block + 1) * WIN, WIN), WIN)
        d_keys = dk_acc[held, :]
        d_keys = (d_keys + pltpu.roll(d_keys, 64, 1)) * score_scale
        d_keys = d_keys * cos_ref[rows, :] - partner(d_keys) * sin_ref[rows, :]
        d_values = dv_acc[held, :]
        d_values = d_values + pltpu.roll(d_values, 64, 1)
        draw_ref[rows, width:] = jnp.where(lane < 64, d_keys, d_values).astype(bf16)
        return carry

    lax.fori_loop(0, tokens // WIN, finish, 0)


def attend_back(split_at, sinks, queries, kv, d_att, lse, cosine, sine):
    tokens, width = queries.shape
    vmem = pl.BlockSpec(memory_space=pltpu.VMEM)
    smem = pl.BlockSpec(memory_space=pltpu.SMEM)
    return pl.pallas_call(
        attend_back_kernel,
        out_shape=(
            jax.ShapeDtypeStruct((tokens, width + LANES), bf16),
            jax.ShapeDtypeStruct((8, LANES), f32),
        ),
        in_specs=[smem, smem, vmem, vmem, vmem, vmem, vmem, vmem],
        out_specs=(vmem, vmem),
        scratch_shapes=[pltpu.VMEM((tokens + WIN, LANES), f32), pltpu.VMEM((tokens + WIN, LANES), f32)],
        compiler_params=pltpu.CompilerParams(vmem_limit_bytes=32 * 2**20),
        cost_estimate=pl.CostEstimate(
            flops=tokens * width * 2 * WIN * 20, bytes_accessed=8 * 2**20, transcendentals=0
        ),
        name="attend_back",
    )(split_at, sinks, queries, kv, d_att, lse, cosine, sine)


def expert_kernel(units, first, *refs):
    experts, capacity, tile = units
    ids_ref, h_ref, g_ref, wg_ref, wu_ref, wd_ref = refs[:6]
    refs = refs[6:] if first else refs[10:]
    back_ref, own_ref, other_ref, x_ref, gr_ref, act_ref, du_ref, xf, gf = refs
    parity = ids_ref[2]
    T = h_ref.shape[2]
    D = wd_ref.shape[1]
    ffp = wd_ref.shape[0]
    at_blocks = [(i, j) for i in range(h_ref.shape[0]) for j in range(h_ref.shape[1])]
    expert = ids_ref[0]
    place_col = ids_ref[1]
    tail = h_ref.shape[3] - LANES
    base = D - tail
    lane = lax.broadcasted_iota(jnp.int32, (T, LANES), 1)
    row = lax.broadcasted_iota(jnp.int32, (T, T), 0)
    col = lax.broadcasted_iota(jnp.int32, (T, T), 1)
    before = jnp.where(col < row, 1.0, 0.0).astype(bf16)
    places = []
    weights = []
    for b, (i, j) in enumerate(at_blocks):
        last = h_ref[i, j, :, tail:].astype(f32)
        hit = jnp.sum(jnp.where(lane == base + 3 * experts + expert, last, 0.0), axis=1, keepdims=True)
        hits = jnp.broadcast_to(hit, (T, LANES))
        slot = matmul(before, hits.astype(bf16))
        place = jnp.where((slot == lane.astype(f32)) & (hits > 0.5), 1.0, 0.0)[:, :capacity].astype(bf16)
        places.append(place)
        at = pl.ds(b * capacity, capacity)
        xf[at, :] = contract_first(place, h_ref[i, j])
        ends = xf[at, tail:]
        lane_c = lax.broadcasted_iota(jnp.int32, ends.shape, 1) - base - expert
        mine = (lane_c == 0) | (lane_c == experts) | (lane_c == 2 * experts)
        weight = jnp.sum(jnp.where(mine, ends, 0.0), axis=1, keepdims=True)
        weights.append(weight)
        gf[at, :] = contract_first(place, g_ref[i, j]) * weight
    x_ref[...] = xf[:, :D].astype(bf16)
    gr_ref[...] = gf[:, :D].astype(bf16)
    weight_all = jnp.concatenate(weights, axis=0)
    share = jnp.zeros_like(weight_all)
    for n in range(ffp // tile):
        at = pl.ds(n * tile, tile)
        at_up = pl.ds(ffp + n * tile, tile)
        gate = matmul(x_ref[...], wg_ref[:, at])
        up = matmul(x_ref[...], wu_ref[:, at])
        d_act = contract_last(gr_ref[...], wd_ref[at, :])
        clipped = jnp.minimum(gate, limit_value)
        up_one = jnp.clip(up, -limit_value, limit_value) + 1.0
        sig = 1.0 / (1.0 + jnp.exp(-alpha_value * clipped))
        swish = clipped * sig
        act = (up_one * swish).astype(bf16)
        act_ref[:, at] = act
        share = share + jnp.sum(act.astype(f32) * d_act, axis=1, keepdims=True)
        d_gate = jnp.where(
            gate < limit_value, d_act * up_one * (sig + alpha_value * swish * (1.0 - sig)), 0.0
        )
        d_up = jnp.where((up > -limit_value) & (up < limit_value), d_act * swish, 0.0)
        du_ref[:, at] = d_gate.astype(bf16)
        du_ref[:, at_up] = d_up.astype(bf16)
    step = 1536
    for start in range(0, D, step):
        size = min(step, D - start)
        d_rows = contract_last(du_ref[:, :ffp], wg_ref[start : start + size, :])
        d_rows = d_rows + contract_last(du_ref[:, ffp:], wu_ref[start : start + size, :])
        for b, (i, j) in enumerate(at_blocks):
            part = d_rows[b * capacity : (b + 1) * capacity].astype(bf16)
            back_ref[i, j, :, start : start + size] = matmul(places[b], part).astype(bf16)
    high = share.astype(bf16).astype(f32)
    spare = back_ref.shape[3] - D
    lane_s = lax.broadcasted_iota(jnp.int32, (capacity, spare), 1)
    for b, (i, j) in enumerate(at_blocks):
        own = slice(b * capacity, (b + 1) * capacity)
        terms = jnp.where(lane_s == place_col, high[own], 0.0)
        terms = jnp.where(lane_s == place_col + 1, share[own] - high[own], terms)
        back_ref[i, j, :, D:] = matmul(places[b], terms.astype(bf16)).astype(bf16)
    groups = h_ref.shape[1]
    if own_ref.shape[3] > D:
        own_ref[0, :, :, D:] = jnp.zeros((groups, T, own_ref.shape[3] - D), bf16)
        other_ref[0, :, :, D:] = jnp.zeros((groups, T, own_ref.shape[3] - D), bf16)
    for start in range(0, D, step):
        size = min(step, D - start)
        rows = matmul(act_ref[...], wd_ref[:, start : start + size]) * weight_all
        for j in range(groups):
            pair = []
            for b in (j, groups + j):
                part = rows[b * capacity : (b + 1) * capacity].astype(bf16)
                pair.append(matmul(places[b], part))
            own_ref[0, j, :, start : start + size] = jnp.where(parity == 0, pair[0], pair[1]).astype(bf16)
            other_ref[0, j, :, start : start + size] = jnp.where(parity == 0, pair[1], pair[0]).astype(bf16)


def run_expert(ids, h_part, g_all, w_gate, w_up, w_down, experts, capacity, spare, half, kept):
    S, FH, T, wide = h_part.shape
    ffp, D = w_down.shape
    lead, deep = 2, min(FH, 2)
    grid = (S // lead, FH // deep)
    tile = 256 if ffp % 256 == 0 else LANES
    rows = lead * deep * capacity
    smem = pl.BlockSpec(memory_space=pltpu.SMEM)
    held = pl.BlockSpec(memory_space=pl.ANY)
    before = half * grid[1]

    def tokens(width, skip=0):
        return pl.BlockSpec((lead, deep, T, width), lambda i, j: (i, j + skip, 0, 0))

    pair = pl.BlockSpec((1, deep, T, wide), lambda i, j: (i, j, 0, 0))

    def slots(width):
        return pl.BlockSpec((rows, width), lambda i, j: ((half * grid[0] + i) * grid[1] + j, 0))

    def whole(shape):
        return pl.BlockSpec(shape, lambda i, j: (0, 0), pipeline_mode=pl.Buffered(1))

    total = 2 * S * FH * capacity
    first = kept is None
    extra = () if first else tuple(kept)
    return pl.pallas_call(
        functools.partial(expert_kernel, (experts, capacity, tile), first),
        grid=grid,
        out_shape=(
            jax.ShapeDtypeStruct((S, FH, T, D + spare), bf16),
            jax.ShapeDtypeStruct((S // 2, FH, T, wide), bf16),
            jax.ShapeDtypeStruct((S // 2, FH, T, wide), bf16),
            jax.ShapeDtypeStruct((total, D), bf16),
            jax.ShapeDtypeStruct((total, D), bf16),
            jax.ShapeDtypeStruct((total, ffp), bf16),
            jax.ShapeDtypeStruct((total, 2 * ffp), bf16),
        ),
        in_specs=[smem, tokens(wide), tokens(wide, before)]
        + [whole(w.shape) for w in (w_gate, w_up, w_down)]
        + [held] * len(extra),
        out_specs=(tokens(D + spare), pair, pair, slots(D), slots(D), slots(ffp), slots(2 * ffp)),
        input_output_aliases={6 + k: 3 + k for k in range(len(extra))},
        scratch_shapes=[pltpu.VMEM((rows, wide), f32)] * 2,
        compiler_params=pltpu.CompilerParams(vmem_limit_bytes=62 * 2**20),
        cost_estimate=pl.CostEstimate(
            flops=total * D * ffp * 6, bytes_accessed=60 * 2**20, transcendentals=0
        ),
        name="experts",
    )(ids, h_part, g_all, w_gate, w_up, w_down, *extra)


def rows_at_once(rows):
    return 144 if rows % 144 == 0 else rows


def cut_kernel(parts, ff, w_ref, gate_ref, up_ref):
    for half, out_ref in enumerate((gate_ref, up_ref)):
        ffp = out_ref.shape[2]
        for part in range(parts):
            first = (half * parts + part) * ff
            out_ref[part, :, :ff] = w_ref[:, first : first + ff]
            if ffp > ff:
                out_ref[part, :, ff:] = jnp.zeros((w_ref.shape[0], ffp - ff), bf16)


def cut_units(w, parts, ff, ffp):
    rows = w.shape[0]
    step = rows_at_once(rows)
    return pl.pallas_call(
        functools.partial(cut_kernel, parts, ff),
        grid=(rows // step,),
        out_shape=(jax.ShapeDtypeStruct((parts, rows, ffp), bf16),) * 2,
        in_specs=[pl.BlockSpec((step, w.shape[1]), lambda i: (i, 0))],
        out_specs=(pl.BlockSpec((parts, step, ffp), lambda i: (0, i, 0)),) * 2,
        compiler_params=pltpu.CompilerParams(vmem_limit_bytes=40 * 2**20),
        cost_estimate=pl.CostEstimate(flops=0, bytes_accessed=4 * w.size, transcendentals=0),
        name="cut_units",
    )(w)


def join_kernel(ff, gate_ref, up_ref, out_ref):
    for half, g_ref in enumerate((gate_ref, up_ref)):
        parts = g_ref.shape[0]
        for part in range(parts):
            first = (half * parts + part) * ff
            out_ref[:, first : first + ff] = g_ref[part, :, :ff].astype(f32)


def join_units(gate, up, ff):
    parts, rows, width = gate.shape
    step = rows_at_once(rows)
    return pl.pallas_call(
        functools.partial(join_kernel, ff),
        grid=(rows // step,),
        out_shape=jax.ShapeDtypeStruct((rows, 2 * parts * ff), f32),
        in_specs=[pl.BlockSpec((parts, step, width), lambda i: (0, i, 0))] * 2,
        out_specs=pl.BlockSpec((step, 2 * parts * ff), lambda i: (i, 0)),
        compiler_params=pltpu.CompilerParams(vmem_limit_bytes=48 * 2**20),
        cost_estimate=pl.CostEstimate(flops=0, bytes_accessed=12 * gate.size, transcendentals=0),
        name="join_units",
    )(gate, up)


def heads_kernel(q_cols, head_dim, g_ref, q_ref, k_ref, v_ref):
    sources = g_ref.shape[0]
    kv_heads = k_ref.shape[1] // head_dim
    repeat = sources // kv_heads
    for source in range(sources):
        q_ref[:, source * q_cols : (source + 1) * q_cols] = g_ref[source, :, :q_cols].astype(f32)
    for out_ref, begin in ((k_ref, q_cols), (v_ref, q_cols + head_dim)):
        for head in range(kv_heads):
            total = g_ref[head * repeat, :, begin : begin + head_dim].astype(f32)
            for other in range(1, repeat):
                total = total + g_ref[head * repeat + other, :, begin : begin + head_dim].astype(f32)
            out_ref[:, head * head_dim : (head + 1) * head_dim] = total


def join_heads(grads, q_cols, head_dim, kv_heads):
    sources, rows, width = grads.shape
    step = rows_at_once(rows)
    kv_cols = kv_heads * head_dim
    return pl.pallas_call(
        functools.partial(heads_kernel, q_cols, head_dim),
        grid=(rows // step,),
        out_shape=(
            jax.ShapeDtypeStruct((rows, sources * q_cols), f32),
            jax.ShapeDtypeStruct((rows, kv_cols), f32),
            jax.ShapeDtypeStruct((rows, kv_cols), f32),
        ),
        in_specs=[pl.BlockSpec((sources, step, width), lambda i: (0, i, 0))],
        out_specs=(
            pl.BlockSpec((step, sources * q_cols), lambda i: (i, 0)),
            pl.BlockSpec((step, kv_cols), lambda i: (i, 0)),
            pl.BlockSpec((step, kv_cols), lambda i: (i, 0)),
        ),
        compiler_params=pltpu.CompilerParams(vmem_limit_bytes=48 * 2**20),
        cost_estimate=pl.CostEstimate(flops=0, bytes_accessed=6 * grads.size, transcendentals=0),
        name="join_heads",
    )(grads)


def gather_direct(value, axis):
    count = lax.axis_size(axis)
    spread = jnp.broadcast_to(value[None], (count,) + value.shape)
    return lax.all_to_all(spread, axis, split_axis=0, concat_axis=0, tiled=True)


def sum_direct(parts, axis):
    got = lax.all_to_all(parts, axis, split_axis=0, concat_axis=0, tiled=True)
    return jnp.sum(got.astype(f32), axis=0)


def shifted(value, axis, steps):
    count = lax.axis_size(axis)
    return lax.ppermute(value, axis, [(i, (i + steps) % count) for i in range(count)])


def taken(parts, index):
    return lax.dynamic_index_in_dim(parts, index, 0, keepdims=False)


def sent(parts, k):
    count = lax.axis_size("fsdp")
    return shifted(taken(parts, (lax.axis_index("fsdp") + k) % count), "fsdp", k)


def placed_parts(parts, got):
    count = lax.axis_size("fsdp")
    for k, piece in got.items():
        parts = lax.dynamic_update_index_in_dim(
            parts, piece, (lax.axis_index("fsdp") - k) % count, 0
        )
    return parts


def summed_parts(parts, got):
    total = taken(parts, lax.axis_index("fsdp")).astype(f32)
    for piece in got:
        total = total + piece.astype(f32)
    return total


def sum_turned(parts, axis):
    total = parts[0].astype(f32)
    for k in range(1, len(parts)):
        total = total + shifted(parts[k], axis, -k).astype(f32)
    return total


def row_major(value):
    return with_layout_constraint(value, Layout(major_to_minor=tuple(range(value.ndim))))


def after(value, *others):
    return lax.optimization_barrier((value,) + others)[0]


def together(*lists):
    flat = lax.optimization_barrier(tuple(item for items in lists for item in items))
    result, at = [], 0
    for items in lists:
        result.append(list(flat[at : at + len(items)]))
        at += len(items)
    return result


def flat_tiles(items, dtype):
    flat = jnp.concatenate([item.reshape(-1) for item in items]).astype(dtype)
    padded = round_up(flat.shape[0], 16 * LANES)
    return jnp.pad(flat, (0, padded - flat.shape[0])).reshape(-1, LANES)


def back_kernel(d_ref, w_ref, x_ref, r_ref, out_ref, gain_ref):
    d_h = contract_last(d_ref[...], w_ref[...])
    out_ref[...] = d_h.astype(bf16)
    sums = jnp.sum(d_h * x_ref[...].astype(f32) * r_ref[...], axis=0, keepdims=True)

    @pl.when(pl.program_id(0) == 0)
    def _():
        gain_ref[...] = jnp.zeros_like(gain_ref)

    gain_ref[...] += jnp.broadcast_to(sums, gain_ref.shape)


def rows_back(d_raw, w_qkv, x_all, r_all):
    rows, width = d_raw.shape
    D = w_qkv.shape[0]
    step = 256
    return pl.pallas_call(
        back_kernel,
        grid=(rows // step,),
        out_shape=(jax.ShapeDtypeStruct((rows, D), bf16), jax.ShapeDtypeStruct((8, D), f32)),
        in_specs=[
            pl.BlockSpec((step, width), lambda i: (i, 0)),
            pl.BlockSpec((D, width), lambda i: (0, 0)),
            pl.BlockSpec((step, D), lambda i: (i, 0)),
            pl.BlockSpec((step, 1), lambda i: (i, 0)),
        ],
        out_specs=(pl.BlockSpec((step, D), lambda i: (i, 0)), pl.BlockSpec((8, D), lambda i: (0, 0))),
        compiler_params=pltpu.CompilerParams(vmem_limit_bytes=40 * 2**20),
        cost_estimate=pl.CostEstimate(
            flops=2 * rows * D * width, bytes_accessed=20 * 2**20, transcendentals=0
        ),
        name="rows_back",
    )(d_raw, w_qkv, x_all, r_all)


def spread_tables(S, F):
    ratio = S // F
    return [[(src, ((src + k) % F) * ratio + src // F) for src in range(S)] for k in range(F)]


def gather_heads(pieces, s, S, F):
    ratio = S // F
    rows = jnp.zeros_like(pieces)
    for k, perm in enumerate(spread_tables(S, F)):
        sent = lax.dynamic_index_in_dim(pieces, (s + k) % F, 0, keepdims=False)
        got = lax.ppermute(sent, "seq", perm)
        rows = lax.dynamic_update_index_in_dim(rows, got, (s // ratio - k) % F, 0)
    return rows


def return_heads(rows, s, S, F):
    ratio = S // F
    got = []
    for k, perm in enumerate(spread_tables(S, F)):
        sent = lax.dynamic_index_in_dim(rows, (s // ratio - k) % F, 0, keepdims=False)
        got.append(lax.ppermute(sent, "seq", [(b, a) for a, b in perm]))
    return got


def return_places(got, s):
    pieces = jnp.broadcast_to(got[0][None], (len(got),) + got[0].shape)
    for k, piece in enumerate(got):
        pieces = lax.dynamic_update_index_in_dim(pieces, piece, (s + k) % len(got), 0)
    return pieces


def local(
    hidden_in,
    out_grad,
    boundary,
    routes,
    gain_one,
    w_query,
    w_key,
    w_value,
    w_output,
    sink_logits,
    gain_two,
    w_router,
    w_in,
    w_out,
):
    S = lax.axis_size("seq")
    F = lax.axis_size("fsdp")
    s = lax.axis_index("seq")
    z = lax.axis_index("fsdp")
    T, D = hidden_in.shape[1:]
    Tg = S * T
    rows_d = w_query.shape[0]
    heads = sink_logits.shape[0] * F
    head_dim = w_query.shape[1] // heads
    kv_heads = w_key.shape[1] // head_dim
    group_size = heads // kv_heads
    heads_own = heads // S
    q_cols = heads_own * head_dim
    experts = w_router.shape[1]
    top_count = routes.shape[2]
    capacity = T * top_count * 9 // (8 * experts)
    ff = w_out.shape[1]
    ffp = round_up(ff, LANES)
    sub = w_output.shape[0] // S
    ratio = S // F

    x_own = hidden_in[0]
    x_all = row_major(lax.all_gather(row_major(x_own), "seq", axis=0, tiled=True))

    kv_head = (s * heads_own) // group_size
    qkv_shard = jnp.concatenate(
        [
            lax.dynamic_slice_in_dim(w_query, s * q_cols, q_cols, 1),
            lax.dynamic_slice_in_dim(w_key, kv_head * head_dim, head_dim, 1),
            lax.dynamic_slice_in_dim(w_value, kv_head * head_dim, head_dim, 1),
        ],
        axis=1,
    )
    w_qkv = lax.all_gather(after(qkv_shard, x_all), "fsdp", axis=0, tiled=True)

    small = flat_tiles((gain_one, gain_two, sink_logits, w_router), bf16)
    small_all = gather_direct(small, "fsdp").reshape(F, -1)
    own_sinks = sink_logits.shape[0]
    cut = [rows_d, 2 * rows_d, 2 * rows_d + own_sinks, 2 * rows_d + own_sinks + rows_d * experts]
    g_one = small_all[:, : cut[0]].reshape(1, D).astype(f32)
    g_two = small_all[:, cut[0] : cut[1]].reshape(1, D).astype(f32)
    sink_all = small_all[:, cut[1] : cut[2]].reshape(heads).astype(f32)
    wr_all = small_all[:, cut[2] : cut[3]].reshape(D, experts)
    sinks = lax.dynamic_slice_in_dim(sink_all, s * heads_own, heads_own, 0)

    split_at = boundary[0]
    token = jnp.arange(Tg, dtype=jnp.int32)
    positions = token - jnp.where(token >= split_at, split_at, 0)
    half_dim = head_dim // 2
    frequency = jnp.exp(-jnp.log(theta_base) * (2.0 * jnp.arange(half_dim, dtype=f32)) / head_dim)
    angles = positions.astype(f32)[:, None] * frequency[None, :]
    cos_half, sin_half = jnp.cos(angles), jnp.sin(angles)
    cosine = jnp.concatenate([cos_half] * 4, axis=1)
    sine = jnp.concatenate([-sin_half, sin_half] * 2, axis=1)

    x_all_f = x_all.astype(f32)
    r_one_all = lax.rsqrt(jnp.mean(x_all_f * x_all_f, axis=1, keepdims=True) + norm_eps)
    h_one = (x_all_f * r_one_all * g_one).astype(bf16)
    wo_sub = lax.dynamic_slice_in_dim(w_output, s * sub, sub, 0)
    wo_pieces = jnp.broadcast_to(wo_sub[None], (F, sub, D))
    for k in range(1, F):
        wo_pieces = lax.dynamic_update_index_in_dim(
            wo_pieces, shifted(wo_sub, "fsdp", k), (z - k) % F, 0
        )
    wo_own = gather_heads(wo_pieces, s, S, F).reshape(F * sub, D)

    half = F // 2
    wide = round_up(D + 4 * experts, LANES)
    near = [1, F - 1]
    far = [k for k in range(1, F) if k not in near]
    d_own = jnp.pad(out_grad[0], ((0, 0), (0, wide - D)))
    cut_gate, cut_up = cut_units(w_in[0], F, ff, ffp)
    w_down = jnp.pad(w_out[0], ((0, ffp - ff), (0, 0)))
    d_own, cut_gate, cut_up, w_down, w_qkv = lax.optimization_barrier(
        (d_own, cut_gate, cut_up, w_down, w_qkv)
    )
    qkv = matmul(h_one, w_qkv)
    queries, kv, attended, lse = attend(boundary, sinks, qkv, cosine, sine, q_cols)
    d_out_got = {k: shifted(d_own, "fsdp", k) for k in near}

    branch_part = row_major(matmul(attended, wo_own).astype(bf16))
    (branch_part, d_own, cut_gate), near_got = together(
        [branch_part, d_own, cut_gate], [d_out_got[k] for k in near]
    )
    d_out_got = dict(zip(near, near_got))
    branch = lax.psum_scatter(branch_part, "seq", scatter_dimension=0, tiled=True)
    far_got = [shifted(d_own, "fsdp", k) for k in far]
    gate_got = {near[0]: sent(cut_gate, near[0])}
    (branch, gate_got[near[0]]), far_got = together([branch, gate_got[near[0]]], far_got)
    d_out_got.update(zip(far, far_got))
    d_stack = row_major(jnp.stack([d_own] + [d_out_got[k] for k in range(1, F)]))

    def over_seq(stack):
        return row_major(lax.all_gather(stack, "seq", axis=0))

    d_out_all = over_seq(d_stack)
    x_f = x_own.astype(f32)
    resid = x_f + branch.astype(f32)
    r_two = lax.rsqrt(jnp.mean(resid * resid, axis=1, keepdims=True) + norm_eps)
    h_two = (resid * r_two * g_two).astype(bf16)

    blocks = S * F
    one_hot = (routes[0][:, :, None] == jnp.arange(experts, dtype=jnp.int32)).astype(f32)
    logits = matmul(h_two, wr_all)
    chosen = jnp.sum(one_hot * logits[:, None, :], axis=2)
    weights = jax.nn.softmax(chosen, axis=1)
    weight_e = jnp.sum(one_hot * weights[:, :, None], axis=1)
    hit_e = jnp.sum(one_hot, axis=1)
    high = lax.reduce_precision(weight_e, 8, 7)
    middle = lax.reduce_precision(weight_e - high, 8, 7)
    low = weight_e - high - middle
    fill = jnp.zeros((T, wide - D - 4 * experts), bf16)
    h_two_wide = jnp.concatenate(
        [h_two] + [part.astype(bf16) for part in (high, middle, low, hit_e)] + [fill], axis=1
    )

    h_two_wide = after(h_two_wide, d_stack)
    h_two_got = [shifted(h_two_wide, "fsdp", k) for k in range(1, F)]
    h_turned = [h_two_wide] + h_two_got
    h_near = row_major(jnp.stack(h_turned[:half]))
    h_far = row_major(jnp.stack(h_turned[half:]))
    h_near, h_far, cut_gate, cut_up = lax.optimization_barrier((h_near, h_far, cut_gate, cut_up))
    gate_far = [sent(cut_gate, k) for k in far]
    gate_far, (h_near, cut_gate, cut_up, d_out_all) = together(
        gate_far, [h_near, cut_gate, cut_up, d_out_all]
    )
    h_parts = [over_seq(h_near)]
    gate_got.update(zip(far, gate_far))
    gate_last, up_first = sent(cut_gate, near[1]), sent(cut_up, near[0])
    gate_last, up_first, h_far, cut_up = lax.optimization_barrier((gate_last, up_first, h_far, cut_up))
    h_parts.append(over_seq(h_far))
    gate_got[near[1]] = gate_last
    up_got = {near[0]: up_first}
    up_got.update({k: sent(cut_up, k) for k in range(1, F) if k not in up_got})
    w_gate = placed_parts(cut_gate, gate_got).reshape(D, ffp)
    w_up = placed_parts(cut_up, up_got).reshape(D, ffp)

    spare = round_up(D + 2 * experts * F, LANES) - D
    ids = jnp.stack([s, 2 * (s * F + z), s % 2])
    def to_group(parts):
        return row_major(lax.psum_scatter(parts, "seq", scatter_dimension=0, tiled=True))[0]

    def swapped(parts):
        return lax.ppermute(parts, "seq", [(i, i ^ 1) for i in range(S)])

    def added(left, right):
        return (left.astype(f32) + right.astype(f32)).astype(bf16)

    def spread_sum(parts):
        pairs = S // 2
        own = taken(parts, s // 2)
        return [own] + [shifted(taken(parts, (s // 2 + k) % pairs), "seq", 2 * k) for k in range(1, pairs)]

    args = (w_gate, w_up, w_down, experts, capacity, spare)
    back, mine, other, *kept = run_expert(ids, h_parts[0], d_out_all, *args, 0, None)
    backs = [to_group(back)]
    back, mine_two, other_two, *kept = run_expert(ids, h_parts[1], d_out_all, *args, 1, kept)
    backs.append(to_group(back))
    rows_x, rows_g, activation, d_units = kept
    other, other_two = swapped(row_major(other)), swapped(row_major(other_two))

    def units_grad(units):
        grad = contract_first(rows_x, units).astype(bf16)
        return row_major(grad).reshape(F, rows_d, ffp)

    grad_gate = units_grad(d_units[:, :ffp])
    gate_first = sent(grad_gate, near[0])
    d_units, gate_first, grad_gate, backs[0], other, other_two = lax.optimization_barrier(
        (d_units, gate_first, grad_gate, backs[0], other, other_two)
    )
    outs = [row_major(added(mine, other)), row_major(added(mine_two, other_two))]
    grad_up = units_grad(d_units[:, ffp:])
    gate_rest = [sent(grad_gate, k) for k in near[1:] + far]
    back_near = [shifted(backs[0][k], "fsdp", -k) for k in range(1, half)]
    grad_down = contract_first(activation, rows_g)[:ff]
    (backs[1], grad_up, grad_down), gate_rest, back_near, outs = together(
        [backs[1], grad_up, grad_down], gate_rest, back_near, outs
    )
    gate_back = dict(zip(near + far, [gate_first] + gate_rest))
    d_wide = backs[0][0].astype(f32)
    for piece in back_near:
        d_wide = d_wide + piece.astype(f32)
    for k in range(half):
        d_wide = d_wide + shifted(backs[1][k], "fsdp", -half - k).astype(f32)
    mix_first = spread_sum(outs[0])
    mix_first, (d_wide, grad_up, outs[1]) = together(mix_first, [d_wide, grad_up, outs[1]])

    d_h_two = d_wide[:, :D]
    share_e = d_wide[:, D : D + 2 * experts * F].reshape(T, experts, 2 * F).sum(axis=2)
    shares = jnp.sum(one_hot * share_e[:, None, :], axis=2)
    d_chosen = shares - weights * jnp.sum(shares, axis=1, keepdims=True)
    d_logits = jnp.sum(one_hot * d_chosen[:, :, None], axis=1).astype(bf16)
    d_h_two = d_h_two + contract_last(d_logits, wr_all)
    grad_router = contract_first(h_two, d_logits)

    d_out = out_grad[0].astype(f32)
    scaled_two = g_two * d_h_two
    d_resid = (
        d_out
        + r_two * scaled_two
        - resid * (r_two * r_two * r_two) * jnp.mean(resid * scaled_two, axis=1, keepdims=True)
    )
    grad_gain_two = jnp.sum(d_h_two * resid * r_two, axis=0)

    d_branch, grad_up = lax.optimization_barrier((row_major(d_resid.astype(bf16)), grad_up))
    d_branch = row_major(lax.all_gather(d_branch, "seq", axis=0, tiled=True))
    up_near = [sent(grad_up, k) for k in near]
    up_near, (d_branch, grad_up, outs[1]) = together(up_near, [d_branch, grad_up, outs[1]])
    up_back = dict(zip(near, up_near))
    up_far = [sent(grad_up, k) for k in far]
    d_att = contract_last(d_branch, wo_own).astype(bf16)
    grad_wo = contract_first(attended, d_branch).astype(bf16).reshape(F, sub, D)
    wo_back = return_heads(row_major(grad_wo), s, S, F)
    d_raw, d_sinks = attend_back(boundary, sinks, queries, kv, d_att, lse, cosine, sine)
    up_far, wo_back, (d_raw, outs[1]) = together(up_far, wo_back, [d_raw, outs[1]])
    up_back.update(zip(far, up_far))
    d_h_part, grad_gain_one = rows_back(d_raw, w_qkv, x_all, r_one_all)
    grad_gain_one = grad_gain_one[0]
    d_raw, d_h_part = lax.optimization_barrier((d_raw, d_h_part))
    d_h_one = lax.psum_scatter(d_h_part, "seq", scatter_dimension=0, tiled=True)
    grad_qkv = contract_first(h_one, d_raw).astype(bf16)
    grad_qkv = row_major(grad_qkv).reshape(F, rows_d, q_cols + 2 * head_dim)
    grad_qkv, d_sinks, mix_first = lax.optimization_barrier((grad_qkv, d_sinks, mix_first))
    qkv_got = [sent(grad_qkv, k) for k in range(1, F)]
    grad_wo = return_places(wo_back, s)
    mix_second = spread_sum(outs[1])
    mixed = sum(piece.astype(f32) for piece in mix_first).astype(bf16)
    mix_got = [shifted(mixed[k], "fsdp", -k) for k in range(1, half)]
    own_heads = jnp.zeros((heads,), f32)
    own_heads = lax.dynamic_update_slice_in_dim(own_heads, d_sinks[0, :heads_own], s * heads_own, 0)
    tiny = jnp.concatenate(
        [
            grad_gain_one.reshape(F, rows_d),
            grad_gain_two.reshape(F, rows_d),
            own_heads.reshape(F, own_sinks),
            grad_router.reshape(F, rows_d * experts),
        ],
        axis=1,
    )
    tiny = jnp.pad(tiny, ((0, 0), (0, round_up(cut[3], 16 * LANES) - cut[3]))).reshape(F, -1, LANES)
    tiny = sum_direct(tiny, "fsdp")
    qkv_got, mix_second, mix_got, (d_h_one, grad_wo, tiny) = together(
        qkv_got, mix_second, mix_got, [d_h_one, grad_wo, tiny]
    )
    grad_qkv = summed_parts(grad_qkv, qkv_got).astype(bf16)
    grad_qkv, grad_wo = lax.optimization_barrier((grad_qkv, grad_wo))
    grad_qkv = lax.all_gather(grad_qkv, "seq", axis=0)
    wo_got = [sent(grad_wo, k) for k in range(1, F)]
    tiny = jnp.sum(gather_direct(tiny, "seq"), axis=0).reshape(-1)
    grad_query, grad_key, grad_value = join_heads(grad_qkv, q_cols, head_dim, kv_heads)
    grad_expert_in = join_units(placed_parts(grad_gate, gate_back), placed_parts(grad_up, up_back), ff)[None]
    d_h_one = d_h_one.astype(f32)
    r_one = lax.rsqrt(jnp.mean(x_f * x_f, axis=1, keepdims=True) + norm_eps)
    scaled_one = g_one * d_h_one
    input_grad = (
        d_resid
        + r_one * scaled_one
        - x_f * (r_one * r_one * r_one) * jnp.mean(x_f * scaled_one, axis=1, keepdims=True)
    )
    wo_got, mix_second, (grad_query, grad_key, grad_value, grad_expert_in, input_grad, tiny) = together(
        wo_got, mix_second, [grad_query, grad_key, grad_value, grad_expert_in, input_grad, tiny]
    )
    grad_wo = summed_parts(grad_wo, wo_got).astype(bf16)
    grad_output = row_major(lax.all_gather(row_major(grad_wo), "seq", axis=0, tiled=True)).astype(f32)

    mixture = mixed[0].astype(f32)
    mixed = sum(piece.astype(f32) for piece in mix_second).astype(bf16)
    for piece in mix_got + [shifted(mixed[k], "fsdp", -half - k) for k in range(half)]:
        mixture = mixture + piece.astype(f32)
    block_out = (resid + mixture[:, :D]).astype(bf16)

    return (
        block_out[None],
        input_grad[None],
        tiny[: cut[0]],
        grad_query,
        grad_key,
        grad_value,
        grad_output,
        tiny[cut[1] : cut[2]],
        tiny[cut[0] : cut[1]],
        tiny[cut[2] : cut[3]].reshape(rows_d, experts),
        grad_expert_in,
        grad_down[None],
    )


def solution(mesh):
    tokens = P("fsdp", "seq", None)
    vector = P("fsdp")
    matrix = P("fsdp", None)
    expert = P("seq", "fsdp", None)
    return jax.shard_map(
        local,
        mesh=mesh,
        in_specs=(
            tokens, tokens, vector, tokens, vector, matrix, matrix, matrix, matrix, vector, vector, matrix, expert, expert,
        ),
        out_specs=(
            tokens, tokens, vector, matrix, matrix, matrix, matrix, vector, vector, matrix, expert, expert,
        ),
        check_vma=False,
    )
```

```python
import functools

import jax
import jax.numpy as jnp
from jax import lax
from jax.experimental import pallas as pl
from jax.experimental.layout import Layout, with_layout_constraint
from jax.experimental.pallas import tpu as pltpu
from jax.sharding import PartitionSpec as P

WIN = 128
LANES = 128

norm_eps = 1e-05
theta_base = 150000.0
limit_value = 7.0
alpha_value = 1.702
score_scale = 0.125

f32 = jnp.float32
bf16 = jnp.bfloat16


def contract_last(left, right):
    return lax.dot_general(left, right, (((1,), (1,)), ((), ())), preferred_element_type=f32)


def contract_first(left, right):
    return lax.dot_general(left, right, (((0,), (0,)), ((), ())), preferred_element_type=f32)


def matmul(left, right):
    return jnp.dot(left, right, preferred_element_type=f32)


def round_up(value, unit):
    return -(-value // unit) * unit


def partner(values):
    lane = lax.broadcasted_iota(jnp.int32, values.shape, 1)
    return jnp.where(lane % 64 < 32, pltpu.roll(values, 96, 1), pltpu.roll(values, 32, 1))


def allowed_keys(block, split_at):
    row = lax.broadcasted_iota(jnp.int32, (WIN, 2 * WIN), 0) + block * WIN
    key = lax.broadcasted_iota(jnp.int32, (WIN, 2 * WIN), 1) + (block - 1) * WIN
    distance = row - key
    return (
        (distance >= 0)
        & (distance < WIN)
        & (key >= 0)
        & ((row >= split_at) == (key >= split_at))
    )


def both_halves(keys_values, low):
    lane = lax.broadcasted_iota(jnp.int32, keys_values.shape, 1)
    other = pltpu.roll(keys_values, 64, 1)
    return jnp.where((lane < 64) == low, keys_values, other)


def attend_kernel(split_ref, sink_ref, qkv_ref, cos_ref, sin_ref, q_ref, kv_ref, att_ref, lse_ref):
    tokens = qkv_ref.shape[0]
    width = q_ref.shape[1]
    pairs = width // LANES
    split_at = split_ref[0]
    lane = lax.broadcasted_iota(jnp.int32, (WIN, LANES), 1)

    def body(block, carry):
        rows = pl.ds(pl.multiple_of(block * WIN, WIN), WIN)
        back = pl.ds(pl.multiple_of(jnp.maximum(block - 1, 0) * WIN, WIN), WIN)
        cosine = cos_ref[rows, :]
        sine = sin_ref[rows, :]
        kv_raw = qkv_ref[rows, width:]
        kv_now = jnp.where(lane < 64, kv_raw * cosine + partner(kv_raw) * sine, kv_raw)
        kv_ref[rows, :] = kv_now.astype(bf16)
        kv_two = jnp.concatenate([kv_ref[back, :].astype(f32), kv_now.astype(bf16).astype(f32)], axis=0)
        keys = both_halves(kv_two, True).astype(bf16)
        values = both_halves(kv_two, False).astype(bf16)
        allowed = allowed_keys(block, split_at)
        stats = jnp.zeros((WIN, LANES), f32)
        for pair in range(pairs):
            at = pl.ds(pair * LANES, LANES)
            raw = qkv_ref[rows, at]
            turned = (raw * cosine + partner(raw) * sine).astype(bf16)
            q_ref[rows, at] = turned
            outs = []
            for half in range(2):
                head = 2 * pair + half
                picked = jnp.where((lane < 64) == (half == 0), turned.astype(f32), 0.0).astype(bf16)
                scores = contract_last(picked, keys) * score_scale
                masked = jnp.where(allowed, scores, -1e30)
                sink = sink_ref[head]
                top = jnp.maximum(jnp.max(masked, axis=1, keepdims=True), sink)
                exps = jnp.where(allowed, jnp.exp(masked - top), 0.0)
                denom = jnp.sum(exps, axis=1, keepdims=True) + jnp.exp(sink - top)
                probs = (exps * (1.0 / denom)).astype(bf16)
                outs.append(matmul(probs, values))
                stats = jnp.where(lane == head, top + jnp.log(denom), stats)
            att_ref[rows, at] = jnp.where(lane < 64, outs[0], outs[1]).astype(bf16)
        lse_ref[rows, :] = stats
        return carry

    lax.fori_loop(0, tokens // WIN, body, 0)


def attend(split_at, sinks, qkv, cosine, sine, width):
    tokens = qkv.shape[0]
    vmem = pl.BlockSpec(memory_space=pltpu.VMEM)
    smem = pl.BlockSpec(memory_space=pltpu.SMEM)
    return pl.pallas_call(
        attend_kernel,
        out_shape=(
            jax.ShapeDtypeStruct((tokens, width), bf16),
            jax.ShapeDtypeStruct((tokens, LANES), bf16),
            jax.ShapeDtypeStruct((tokens, width), bf16),
            jax.ShapeDtypeStruct((tokens, LANES), f32),
        ),
        in_specs=[smem, smem, vmem, vmem, vmem],
        out_specs=(vmem, vmem, vmem, vmem),
        compiler_params=pltpu.CompilerParams(vmem_limit_bytes=32 * 2**20),
        cost_estimate=pl.CostEstimate(
            flops=tokens * width * 2 * WIN * 8, bytes_accessed=8 * 2**20, transcendentals=0
        ),
        name="attend",
    )(split_at, sinks, qkv, cosine, sine)


def attend_back_kernel(
    split_ref, sink_ref, q_ref, kv_ref, datt_ref, lse_ref, cos_ref, sin_ref, draw_ref, dsink_ref, dk_acc, dv_acc
):
    tokens = q_ref.shape[0]
    width = q_ref.shape[1]
    pairs = width // LANES
    split_at = split_ref[0]
    lane = lax.broadcasted_iota(jnp.int32, (WIN, LANES), 1)
    lane_row = lax.broadcasted_iota(jnp.int32, (8, LANES), 1)
    dk_acc[...] = jnp.zeros_like(dk_acc)
    dv_acc[...] = jnp.zeros_like(dv_acc)

    def body(block, sink_sum):
        rows = pl.ds(pl.multiple_of(block * WIN, WIN), WIN)
        back = pl.ds(pl.multiple_of(jnp.maximum(block - 1, 0) * WIN, WIN), WIN)
        both = pl.ds(pl.multiple_of(block * WIN, WIN), 2 * WIN)
        cosine = cos_ref[rows, :]
        sine = sin_ref[rows, :]
        kv_two = jnp.concatenate([kv_ref[back, :], kv_ref[rows, :]], axis=0).astype(f32)
        keys = both_halves(kv_two, True).astype(bf16)
        values = both_halves(kv_two, False).astype(bf16)
        allowed = allowed_keys(block, split_at)
        stats = lse_ref[rows, :]
        d_keys = jnp.zeros((2 * WIN, LANES), f32)
        d_values = jnp.zeros((2 * WIN, LANES), f32)
        for pair in range(pairs):
            at = pl.ds(pair * LANES, LANES)
            turned = q_ref[rows, at].astype(f32)
            d_out = datt_ref[rows, at].astype(f32)
            d_turned = []
            for half in range(2):
                head = 2 * pair + half
                mine = (lane < 64) == (half == 0)
                picked = jnp.where(mine, turned, 0.0).astype(bf16)
                d_picked = jnp.where(mine, d_out, 0.0).astype(bf16)
                total = stats[:, head : head + 1]
                scores = contract_last(picked, keys) * score_scale
                probs = jnp.where(allowed, jnp.exp(scores - total), 0.0)
                d_probs = contract_last(d_picked, values)
                delta = jnp.sum(probs * d_probs, axis=1, keepdims=True)
                d_scores = (probs * (d_probs - delta)).astype(bf16)
                share = jnp.sum(jnp.exp(sink_ref[head] - total) * delta)
                sink_sum = sink_sum - jnp.where(lane_row == head, share, 0.0)
                d_turned.append(matmul(d_scores, keys))
                d_keys = d_keys + contract_first(d_scores, picked)
                d_values = d_values + contract_first(probs.astype(bf16), d_picked)
            d_query = jnp.where(lane < 64, d_turned[0], d_turned[1]) * score_scale
            draw_ref[rows, at] = (d_query * cosine - partner(d_query) * sine).astype(bf16)
        dk_acc[both, :] += d_keys
        dv_acc[both, :] += d_values
        return sink_sum

    dsink_ref[...] = lax.fori_loop(0, tokens // WIN, body, jnp.zeros((8, LANES), f32))

    def finish(block, carry):
        rows = pl.ds(pl.multiple_of(block * WIN, WIN), WIN)
        held = pl.ds(pl.multiple_of((block + 1) * WIN, WIN), WIN)
        d_keys = dk_acc[held, :]
        d_keys = (d_keys + pltpu.roll(d_keys, 64, 1)) * score_scale
        d_keys = d_keys * cos_ref[rows, :] - partner(d_keys) * sin_ref[rows, :]
        d_values = dv_acc[held, :]
        d_values = d_values + pltpu.roll(d_values, 64, 1)
        draw_ref[rows, width:] = jnp.where(lane < 64, d_keys, d_values).astype(bf16)
        return carry

    lax.fori_loop(0, tokens // WIN, finish, 0)


def attend_back(split_at, sinks, queries, kv, d_att, lse, cosine, sine):
    tokens, width = queries.shape
    vmem = pl.BlockSpec(memory_space=pltpu.VMEM)
    smem = pl.BlockSpec(memory_space=pltpu.SMEM)
    return pl.pallas_call(
        attend_back_kernel,
        out_shape=(
            jax.ShapeDtypeStruct((tokens, width + LANES), bf16),
            jax.ShapeDtypeStruct((8, LANES), f32),
        ),
        in_specs=[smem, smem, vmem, vmem, vmem, vmem, vmem, vmem],
        out_specs=(vmem, vmem),
        scratch_shapes=[pltpu.VMEM((tokens + WIN, LANES), f32), pltpu.VMEM((tokens + WIN, LANES), f32)],
        compiler_params=pltpu.CompilerParams(vmem_limit_bytes=32 * 2**20),
        cost_estimate=pl.CostEstimate(
            flops=tokens * width * 2 * WIN * 20, bytes_accessed=8 * 2**20, transcendentals=0
        ),
        name="attend_back",
    )(split_at, sinks, queries, kv, d_att, lse, cosine, sine)


def expert_kernel(units, first, *refs):
    experts, capacity, tile = units
    ids_ref, h_ref, g_ref, wg_ref, wu_ref, wd_ref = refs[:6]
    refs = refs[6:] if first else refs[10:]
    back_ref, own_ref, other_ref, x_ref, gr_ref, act_ref, du_ref, xf, gf = refs
    parity = ids_ref[2]
    T = h_ref.shape[2]
    D = wd_ref.shape[1]
    ffp = wd_ref.shape[0]
    at_blocks = [(i, j) for i in range(h_ref.shape[0]) for j in range(h_ref.shape[1])]
    expert = ids_ref[0]
    place_col = ids_ref[1]
    tail = h_ref.shape[3] - LANES
    base = D - tail
    lane = lax.broadcasted_iota(jnp.int32, (T, LANES), 1)
    row = lax.broadcasted_iota(jnp.int32, (T, T), 0)
    col = lax.broadcasted_iota(jnp.int32, (T, T), 1)
    before = jnp.where(col < row, 1.0, 0.0).astype(bf16)
    places = []
    weights = []
    for b, (i, j) in enumerate(at_blocks):
        last = h_ref[i, j, :, tail:].astype(f32)
        hit = jnp.sum(jnp.where(lane == base + 3 * experts + expert, last, 0.0), axis=1, keepdims=True)
        hits = jnp.broadcast_to(hit, (T, LANES))
        slot = matmul(before, hits.astype(bf16))
        place = jnp.where((slot == lane.astype(f32)) & (hits > 0.5), 1.0, 0.0)[:, :capacity].astype(bf16)
        places.append(place)
        at = pl.ds(b * capacity, capacity)
        xf[at, :] = contract_first(place, h_ref[i, j])
        ends = xf[at, tail:]
        lane_c = lax.broadcasted_iota(jnp.int32, ends.shape, 1) - base - expert
        mine = (lane_c == 0) | (lane_c == experts) | (lane_c == 2 * experts)
        weight = jnp.sum(jnp.where(mine, ends, 0.0), axis=1, keepdims=True)
        weights.append(weight)
        gf[at, :] = contract_first(place, g_ref[i, j]) * weight
    x_ref[...] = xf[:, :D].astype(bf16)
    gr_ref[...] = gf[:, :D].astype(bf16)
    weight_all = jnp.concatenate(weights, axis=0)
    share = jnp.zeros_like(weight_all)
    for n in range(ffp // tile):
        at = pl.ds(n * tile, tile)
        at_up = pl.ds(ffp + n * tile, tile)
        gate = matmul(x_ref[...], wg_ref[:, at])
        up = matmul(x_ref[...], wu_ref[:, at])
        d_act = contract_last(gr_ref[...], wd_ref[at, :])
        clipped = jnp.minimum(gate, limit_value)
        up_one = jnp.clip(up, -limit_value, limit_value) + 1.0
        sig = 1.0 / (1.0 + jnp.exp(-alpha_value * clipped))
        swish = clipped * sig
        act = (up_one * swish).astype(bf16)
        act_ref[:, at] = act
        share = share + jnp.sum(act.astype(f32) * d_act, axis=1, keepdims=True)
        d_gate = jnp.where(
            gate < limit_value, d_act * up_one * (sig + alpha_value * swish * (1.0 - sig)), 0.0
        )
        d_up = jnp.where((up > -limit_value) & (up < limit_value), d_act * swish, 0.0)
        du_ref[:, at] = d_gate.astype(bf16)
        du_ref[:, at_up] = d_up.astype(bf16)
    step = 1536
    for start in range(0, D, step):
        size = min(step, D - start)
        d_rows = contract_last(du_ref[:, :ffp], wg_ref[start : start + size, :])
        d_rows = d_rows + contract_last(du_ref[:, ffp:], wu_ref[start : start + size, :])
        for b, (i, j) in enumerate(at_blocks):
            part = d_rows[b * capacity : (b + 1) * capacity].astype(bf16)
            back_ref[i, j, :, start : start + size] = matmul(places[b], part).astype(bf16)
    high = share.astype(bf16).astype(f32)
    spare = back_ref.shape[3] - D
    lane_s = lax.broadcasted_iota(jnp.int32, (capacity, spare), 1)
    for b, (i, j) in enumerate(at_blocks):
        own = slice(b * capacity, (b + 1) * capacity)
        terms = jnp.where(lane_s == place_col, high[own], 0.0)
        terms = jnp.where(lane_s == place_col + 1, share[own] - high[own], terms)
        back_ref[i, j, :, D:] = matmul(places[b], terms.astype(bf16)).astype(bf16)
    groups = h_ref.shape[1]
    if own_ref.shape[3] > D:
        own_ref[0, :, :, D:] = jnp.zeros((groups, T, own_ref.shape[3] - D), bf16)
        other_ref[0, :, :, D:] = jnp.zeros((groups, T, own_ref.shape[3] - D), bf16)
    for start in range(0, D, step):
        size = min(step, D - start)
        rows = matmul(act_ref[...], wd_ref[:, start : start + size]) * weight_all
        for j in range(groups):
            pair = []
            for b in (j, groups + j):
                part = rows[b * capacity : (b + 1) * capacity].astype(bf16)
                pair.append(matmul(places[b], part))
            own_ref[0, j, :, start : start + size] = jnp.where(parity == 0, pair[0], pair[1]).astype(bf16)
            other_ref[0, j, :, start : start + size] = jnp.where(parity == 0, pair[1], pair[0]).astype(bf16)


def run_expert(ids, h_part, g_all, w_gate, w_up, w_down, experts, capacity, spare, half, kept):
    S, FH, T, wide = h_part.shape
    ffp, D = w_down.shape
    lead, deep = 2, min(FH, 2)
    grid = (S // lead, FH // deep)
    tile = 256 if ffp % 256 == 0 else LANES
    rows = lead * deep * capacity
    smem = pl.BlockSpec(memory_space=pltpu.SMEM)
    held = pl.BlockSpec(memory_space=pl.ANY)
    before = half * grid[1]

    def tokens(width, skip=0):
        return pl.BlockSpec((lead, deep, T, width), lambda i, j: (i, j + skip, 0, 0))

    pair = pl.BlockSpec((1, deep, T, wide), lambda i, j: (i, j, 0, 0))

    def slots(width):
        return pl.BlockSpec((rows, width), lambda i, j: ((half * grid[0] + i) * grid[1] + j, 0))

    def whole(shape):
        return pl.BlockSpec(shape, lambda i, j: (0, 0), pipeline_mode=pl.Buffered(1))

    total = 2 * S * FH * capacity
    first = kept is None
    extra = () if first else tuple(kept)
    return pl.pallas_call(
        functools.partial(expert_kernel, (experts, capacity, tile), first),
        grid=grid,
        out_shape=(
            jax.ShapeDtypeStruct((S, FH, T, D + spare), bf16),
            jax.ShapeDtypeStruct((S // 2, FH, T, wide), bf16),
            jax.ShapeDtypeStruct((S // 2, FH, T, wide), bf16),
            jax.ShapeDtypeStruct((total, D), bf16),
            jax.ShapeDtypeStruct((total, D), bf16),
            jax.ShapeDtypeStruct((total, ffp), bf16),
            jax.ShapeDtypeStruct((total, 2 * ffp), bf16),
        ),
        in_specs=[smem, tokens(wide), tokens(wide, before)]
        + [whole(w.shape) for w in (w_gate, w_up, w_down)]
        + [held] * len(extra),
        out_specs=(tokens(D + spare), pair, pair, slots(D), slots(D), slots(ffp), slots(2 * ffp)),
        input_output_aliases={6 + k: 3 + k for k in range(len(extra))},
        scratch_shapes=[pltpu.VMEM((rows, wide), f32)] * 2,
        compiler_params=pltpu.CompilerParams(vmem_limit_bytes=62 * 2**20),
        cost_estimate=pl.CostEstimate(
            flops=total * D * ffp * 6, bytes_accessed=60 * 2**20, transcendentals=0
        ),
        name="experts",
    )(ids, h_part, g_all, w_gate, w_up, w_down, *extra)


def rows_at_once(rows):
    return 144 if rows % 144 == 0 else rows


def cut_kernel(parts, ff, w_ref, gate_ref, up_ref):
    for half, out_ref in enumerate((gate_ref, up_ref)):
        ffp = out_ref.shape[2]
        for part in range(parts):
            first = (half * parts + part) * ff
            out_ref[part, :, :ff] = w_ref[:, first : first + ff]
            if ffp > ff:
                out_ref[part, :, ff:] = jnp.zeros((w_ref.shape[0], ffp - ff), bf16)


def cut_units(w, parts, ff, ffp):
    rows = w.shape[0]
    step = rows_at_once(rows)
    return pl.pallas_call(
        functools.partial(cut_kernel, parts, ff),
        grid=(rows // step,),
        out_shape=(jax.ShapeDtypeStruct((parts, rows, ffp), bf16),) * 2,
        in_specs=[pl.BlockSpec((step, w.shape[1]), lambda i: (i, 0))],
        out_specs=(pl.BlockSpec((parts, step, ffp), lambda i: (0, i, 0)),) * 2,
        compiler_params=pltpu.CompilerParams(vmem_limit_bytes=40 * 2**20),
        cost_estimate=pl.CostEstimate(flops=0, bytes_accessed=4 * w.size, transcendentals=0),
        name="cut_units",
    )(w)


def join_kernel(ff, gate_ref, up_ref, out_ref):
    for half, g_ref in enumerate((gate_ref, up_ref)):
        parts = g_ref.shape[0]
        for part in range(parts):
            first = (half * parts + part) * ff
            out_ref[:, first : first + ff] = g_ref[part, :, :ff].astype(f32)


def join_units(gate, up, ff):
    parts, rows, width = gate.shape
    step = rows_at_once(rows)
    return pl.pallas_call(
        functools.partial(join_kernel, ff),
        grid=(rows // step,),
        out_shape=jax.ShapeDtypeStruct((rows, 2 * parts * ff), f32),
        in_specs=[pl.BlockSpec((parts, step, width), lambda i: (0, i, 0))] * 2,
        out_specs=pl.BlockSpec((step, 2 * parts * ff), lambda i: (i, 0)),
        compiler_params=pltpu.CompilerParams(vmem_limit_bytes=48 * 2**20),
        cost_estimate=pl.CostEstimate(flops=0, bytes_accessed=12 * gate.size, transcendentals=0),
        name="join_units",
    )(gate, up)


def heads_kernel(q_cols, head_dim, g_ref, q_ref, k_ref, v_ref):
    sources = g_ref.shape[0]
    kv_heads = k_ref.shape[1] // head_dim
    repeat = sources // kv_heads
    for source in range(sources):
        q_ref[:, source * q_cols : (source + 1) * q_cols] = g_ref[source, :, :q_cols].astype(f32)
    for out_ref, begin in ((k_ref, q_cols), (v_ref, q_cols + head_dim)):
        for head in range(kv_heads):
            total = g_ref[head * repeat, :, begin : begin + head_dim].astype(f32)
            for other in range(1, repeat):
                total = total + g_ref[head * repeat + other, :, begin : begin + head_dim].astype(f32)
            out_ref[:, head * head_dim : (head + 1) * head_dim] = total


def join_heads(grads, q_cols, head_dim, kv_heads):
    sources, rows, width = grads.shape
    step = rows_at_once(rows)
    kv_cols = kv_heads * head_dim
    return pl.pallas_call(
        functools.partial(heads_kernel, q_cols, head_dim),
        grid=(rows // step,),
        out_shape=(
            jax.ShapeDtypeStruct((rows, sources * q_cols), f32),
            jax.ShapeDtypeStruct((rows, kv_cols), f32),
            jax.ShapeDtypeStruct((rows, kv_cols), f32),
        ),
        in_specs=[pl.BlockSpec((sources, step, width), lambda i: (0, i, 0))],
        out_specs=(
            pl.BlockSpec((step, sources * q_cols), lambda i: (i, 0)),
            pl.BlockSpec((step, kv_cols), lambda i: (i, 0)),
            pl.BlockSpec((step, kv_cols), lambda i: (i, 0)),
        ),
        compiler_params=pltpu.CompilerParams(vmem_limit_bytes=48 * 2**20),
        cost_estimate=pl.CostEstimate(flops=0, bytes_accessed=6 * grads.size, transcendentals=0),
        name="join_heads",
    )(grads)


def gather_direct(value, axis):
    count = lax.axis_size(axis)
    spread = jnp.broadcast_to(value[None], (count,) + value.shape)
    return lax.all_to_all(spread, axis, split_axis=0, concat_axis=0, tiled=True)


def sum_direct(parts, axis):
    got = lax.all_to_all(parts, axis, split_axis=0, concat_axis=0, tiled=True)
    return jnp.sum(got.astype(f32), axis=0)


def shifted(value, axis, steps):
    count = lax.axis_size(axis)
    return lax.ppermute(value, axis, [(i, (i + steps) % count) for i in range(count)])


def taken(parts, index):
    return lax.dynamic_index_in_dim(parts, index, 0, keepdims=False)


def sent(parts, k):
    count = lax.axis_size("fsdp")
    return shifted(taken(parts, (lax.axis_index("fsdp") + k) % count), "fsdp", k)


def placed_parts(parts, got):
    count = lax.axis_size("fsdp")
    for k, piece in got.items():
        parts = lax.dynamic_update_index_in_dim(
            parts, piece, (lax.axis_index("fsdp") - k) % count, 0
        )
    return parts


def summed_parts(parts, got):
    total = taken(parts, lax.axis_index("fsdp")).astype(f32)
    for piece in got:
        total = total + piece.astype(f32)
    return total


def sum_turned(parts, axis):
    total = parts[0].astype(f32)
    for k in range(1, len(parts)):
        total = total + shifted(parts[k], axis, -k).astype(f32)
    return total


def row_major(value):
    return with_layout_constraint(value, Layout(major_to_minor=tuple(range(value.ndim))))


def after(value, *others):
    return lax.optimization_barrier((value,) + others)[0]


def together(*lists):
    flat = lax.optimization_barrier(tuple(item for items in lists for item in items))
    result, at = [], 0
    for items in lists:
        result.append(list(flat[at : at + len(items)]))
        at += len(items)
    return result


def flat_tiles(items, dtype):
    flat = jnp.concatenate([item.reshape(-1) for item in items]).astype(dtype)
    padded = round_up(flat.shape[0], 16 * LANES)
    return jnp.pad(flat, (0, padded - flat.shape[0])).reshape(-1, LANES)


def back_kernel(d_ref, w_ref, x_ref, r_ref, out_ref, gain_ref):
    d_h = contract_last(d_ref[...], w_ref[...])
    out_ref[...] = d_h.astype(bf16)
    sums = jnp.sum(d_h * x_ref[...].astype(f32) * r_ref[...], axis=0, keepdims=True)

    @pl.when(pl.program_id(0) == 0)
    def _():
        gain_ref[...] = jnp.zeros_like(gain_ref)

    gain_ref[...] += jnp.broadcast_to(sums, gain_ref.shape)


def rows_back(d_raw, w_qkv, x_all, r_all):
    rows, width = d_raw.shape
    D = w_qkv.shape[0]
    step = 256
    return pl.pallas_call(
        back_kernel,
        grid=(rows // step,),
        out_shape=(jax.ShapeDtypeStruct((rows, D), bf16), jax.ShapeDtypeStruct((8, D), f32)),
        in_specs=[
            pl.BlockSpec((step, width), lambda i: (i, 0)),
            pl.BlockSpec((D, width), lambda i: (0, 0)),
            pl.BlockSpec((step, D), lambda i: (i, 0)),
            pl.BlockSpec((step, 1), lambda i: (i, 0)),
        ],
        out_specs=(pl.BlockSpec((step, D), lambda i: (i, 0)), pl.BlockSpec((8, D), lambda i: (0, 0))),
        compiler_params=pltpu.CompilerParams(vmem_limit_bytes=40 * 2**20),
        cost_estimate=pl.CostEstimate(
            flops=2 * rows * D * width, bytes_accessed=20 * 2**20, transcendentals=0
        ),
        name="rows_back",
    )(d_raw, w_qkv, x_all, r_all)


def spread_tables(S, F):
    ratio = S // F
    return [[(src, ((src + k) % F) * ratio + src // F) for src in range(S)] for k in range(F)]


def gather_heads(pieces, s, S, F):
    ratio = S // F
    rows = jnp.zeros_like(pieces)
    for k, perm in enumerate(spread_tables(S, F)):
        sent = lax.dynamic_index_in_dim(pieces, (s + k) % F, 0, keepdims=False)
        got = lax.ppermute(sent, "seq", perm)
        rows = lax.dynamic_update_index_in_dim(rows, got, (s // ratio - k) % F, 0)
    return rows


def return_heads(rows, s, S, F):
    ratio = S // F
    got = []
    for k, perm in enumerate(spread_tables(S, F)):
        sent = lax.dynamic_index_in_dim(rows, (s // ratio - k) % F, 0, keepdims=False)
        got.append(lax.ppermute(sent, "seq", [(b, a) for a, b in perm]))
    return got


def return_places(got, s):
    pieces = jnp.broadcast_to(got[0][None], (len(got),) + got[0].shape)
    for k, piece in enumerate(got):
        pieces = lax.dynamic_update_index_in_dim(pieces, piece, (s + k) % len(got), 0)
    return pieces


def local(
    hidden_in,
    out_grad,
    boundary,
    routes,
    gain_one,
    w_query,
    w_key,
    w_value,
    w_output,
    sink_logits,
    gain_two,
    w_router,
    w_in,
    w_out,
):
    S = lax.axis_size("seq")
    F = lax.axis_size("fsdp")
    s = lax.axis_index("seq")
    z = lax.axis_index("fsdp")
    T, D = hidden_in.shape[1:]
    Tg = S * T
    rows_d = w_query.shape[0]
    heads = sink_logits.shape[0] * F
    head_dim = w_query.shape[1] // heads
    kv_heads = w_key.shape[1] // head_dim
    group_size = heads // kv_heads
    heads_own = heads // S
    q_cols = heads_own * head_dim
    experts = w_router.shape[1]
    top_count = routes.shape[2]
    capacity = T * top_count * 9 // (8 * experts)
    ff = w_out.shape[1]
    ffp = round_up(ff, LANES)
    sub = w_output.shape[0] // S
    ratio = S // F

    x_own = hidden_in[0]
    x_all = row_major(lax.all_gather(row_major(x_own), "seq", axis=0, tiled=True))

    kv_head = (s * heads_own) // group_size
    qkv_shard = jnp.concatenate(
        [
            lax.dynamic_slice_in_dim(w_query, s * q_cols, q_cols, 1),
            lax.dynamic_slice_in_dim(w_key, kv_head * head_dim, head_dim, 1),
            lax.dynamic_slice_in_dim(w_value, kv_head * head_dim, head_dim, 1),
        ],
        axis=1,
    )
    w_qkv = lax.all_gather(after(qkv_shard, x_all), "fsdp", axis=0, tiled=True)

    small = flat_tiles((gain_one, gain_two, sink_logits, w_router), bf16)
    small_all = gather_direct(small, "fsdp").reshape(F, -1)
    own_sinks = sink_logits.shape[0]
    cut = [rows_d, 2 * rows_d, 2 * rows_d + own_sinks, 2 * rows_d + own_sinks + rows_d * experts]
    g_one = small_all[:, : cut[0]].reshape(1, D).astype(f32)
    g_two = small_all[:, cut[0] : cut[1]].reshape(1, D).astype(f32)
    sink_all = small_all[:, cut[1] : cut[2]].reshape(heads).astype(f32)
    wr_all = small_all[:, cut[2] : cut[3]].reshape(D, experts)
    sinks = lax.dynamic_slice_in_dim(sink_all, s * heads_own, heads_own, 0)

    split_at = boundary[0]
    token = jnp.arange(Tg, dtype=jnp.int32)
    positions = token - jnp.where(token >= split_at, split_at, 0)
    half_dim = head_dim // 2
    frequency = jnp.exp(-jnp.log(theta_base) * (2.0 * jnp.arange(half_dim, dtype=f32)) / head_dim)
    angles = positions.astype(f32)[:, None] * frequency[None, :]
    cos_half, sin_half = jnp.cos(angles), jnp.sin(angles)
    cosine = jnp.concatenate([cos_half] * 4, axis=1)
    sine = jnp.concatenate([-sin_half, sin_half] * 2, axis=1)

    x_all_f = x_all.astype(f32)
    r_one_all = lax.rsqrt(jnp.mean(x_all_f * x_all_f, axis=1, keepdims=True) + norm_eps)
    h_one = (x_all_f * r_one_all * g_one).astype(bf16)
    wo_sub = lax.dynamic_slice_in_dim(w_output, s * sub, sub, 0)
    wo_pieces = jnp.broadcast_to(wo_sub[None], (F, sub, D))
    for k in range(1, F):
        wo_pieces = lax.dynamic_update_index_in_dim(
            wo_pieces, shifted(wo_sub, "fsdp", k), (z - k) % F, 0
        )
    wo_own = gather_heads(wo_pieces, s, S, F).reshape(F * sub, D)

    half = F // 2
    wide = round_up(D + 4 * experts, LANES)
    near = [1, F - 1]
    far = [k for k in range(1, F) if k not in near]
    d_own = jnp.pad(out_grad[0], ((0, 0), (0, wide - D)))
    cut_gate, cut_up = cut_units(w_in[0], F, ff, ffp)
    w_down = jnp.pad(w_out[0], ((0, ffp - ff), (0, 0)))
    d_own, cut_gate, cut_up, w_down, w_qkv = lax.optimization_barrier(
        (d_own, cut_gate, cut_up, w_down, w_qkv)
    )
    qkv = matmul(h_one, w_qkv)
    queries, kv, attended, lse = attend(boundary, sinks, qkv, cosine, sine, q_cols)
    d_out_got = {k: shifted(d_own, "fsdp", k) for k in near}

    branch_part = row_major(matmul(attended, wo_own).astype(bf16))
    (branch_part, d_own, cut_gate), near_got = together(
        [branch_part, d_own, cut_gate], [d_out_got[k] for k in near]
    )
    d_out_got = dict(zip(near, near_got))
    branch = lax.psum_scatter(branch_part, "seq", scatter_dimension=0, tiled=True)
    far_got = [shifted(d_own, "fsdp", k) for k in far]
    gate_got = {near[0]: sent(cut_gate, near[0])}
    (branch, gate_got[near[0]]), far_got = together([branch, gate_got[near[0]]], far_got)
    d_out_got.update(zip(far, far_got))
    d_stack = row_major(jnp.stack([d_own] + [d_out_got[k] for k in range(1, F)]))

    def over_seq(stack):
        return row_major(lax.all_gather(stack, "seq", axis=0))

    d_out_all = over_seq(d_stack)
    x_f = x_own.astype(f32)
    resid = x_f + branch.astype(f32)
    r_two = lax.rsqrt(jnp.mean(resid * resid, axis=1, keepdims=True) + norm_eps)
    h_two = (resid * r_two * g_two).astype(bf16)

    blocks = S * F
    one_hot = (routes[0][:, :, None] == jnp.arange(experts, dtype=jnp.int32)).astype(f32)
    logits = matmul(h_two, wr_all)
    chosen = jnp.sum(one_hot * logits[:, None, :], axis=2)
    weights = jax.nn.softmax(chosen, axis=1)
    weight_e = jnp.sum(one_hot * weights[:, :, None], axis=1)
    hit_e = jnp.sum(one_hot, axis=1)
    high = lax.reduce_precision(weight_e, 8, 7)
    middle = lax.reduce_precision(weight_e - high, 8, 7)
    low = weight_e - high - middle
    fill = jnp.zeros((T, wide - D - 4 * experts), bf16)
    h_two_wide = jnp.concatenate(
        [h_two] + [part.astype(bf16) for part in (high, middle, low, hit_e)] + [fill], axis=1
    )

    h_two_wide, d_stack, cut_gate = lax.optimization_barrier((h_two_wide, d_stack, cut_gate))
    h_two_got = [shifted(h_two_wide, "fsdp", k) for k in range(1, F)]
    gate_far = [sent(cut_gate, k) for k in far]
    h_two_got, gate_far, (cut_gate, cut_up) = together(h_two_got, gate_far, [cut_gate, cut_up])
    h_turned = [h_two_wide] + h_two_got
    h_near = row_major(jnp.stack(h_turned[:half]))
    h_far = row_major(jnp.stack(h_turned[half:]))
    h_near, d_out_all = lax.optimization_barrier((h_near, d_out_all))
    h_parts = [over_seq(h_near)]
    gate_got.update(zip(far, gate_far))
    gate_last, up_first = sent(cut_gate, near[1]), sent(cut_up, near[0])
    gate_last, up_first, h_far, cut_up = lax.optimization_barrier((gate_last, up_first, h_far, cut_up))
    h_parts.append(over_seq(h_far))
    gate_got[near[1]] = gate_last
    up_got = {near[0]: up_first}
    up_got.update({k: sent(cut_up, k) for k in range(1, F) if k not in up_got})
    w_gate = placed_parts(cut_gate, gate_got).reshape(D, ffp)
    w_up = placed_parts(cut_up, up_got).reshape(D, ffp)

    spare = round_up(D + 2 * experts * F, LANES) - D
    ids = jnp.stack([s, 2 * (s * F + z), s % 2])
    def to_group(parts):
        return row_major(lax.psum_scatter(parts, "seq", scatter_dimension=0, tiled=True))[0]

    def swapped(parts):
        return lax.ppermute(parts, "seq", [(i, i ^ 1) for i in range(S)])

    def added(left, right):
        return (left.astype(f32) + right.astype(f32)).astype(bf16)

    def spread_sum(parts):
        pairs = S // 2
        own = taken(parts, s // 2)
        return [own] + [shifted(taken(parts, (s // 2 + k) % pairs), "seq", 2 * k) for k in range(1, pairs)]

    args = (w_gate, w_up, w_down, experts, capacity, spare)
    back, mine, other, *kept = run_expert(ids, h_parts[0], d_out_all, *args, 0, None)
    backs = [to_group(back)]
    back, mine_two, other_two, *kept = run_expert(ids, h_parts[1], d_out_all, *args, 1, kept)
    backs.append(to_group(back))
    rows_x, rows_g, activation, d_units = kept
    other, other_two = swapped(row_major(other)), swapped(row_major(other_two))

    def units_grad(units):
        grad = contract_first(rows_x, units).astype(bf16)
        return row_major(grad).reshape(F, rows_d, ffp)

    grad_gate = units_grad(d_units[:, :ffp])
    gate_first = sent(grad_gate, near[0])
    d_units, gate_first, grad_gate, backs[0], other, other_two = lax.optimization_barrier(
        (d_units, gate_first, grad_gate, backs[0], other, other_two)
    )
    outs = [row_major(added(mine, other)), row_major(added(mine_two, other_two))]
    grad_up = units_grad(d_units[:, ffp:])
    gate_rest = [sent(grad_gate, k) for k in near[1:] + far]
    back_near = [shifted(backs[0][k], "fsdp", -k) for k in range(1, half)]
    grad_down = contract_first(activation, rows_g)[:ff]
    (backs[1], grad_up, grad_down), gate_rest, back_near, outs = together(
        [backs[1], grad_up, grad_down], gate_rest, back_near, outs
    )
    gate_back = dict(zip(near + far, [gate_first] + gate_rest))
    d_wide = backs[0][0].astype(f32)
    for piece in back_near:
        d_wide = d_wide + piece.astype(f32)
    for k in range(half):
        d_wide = d_wide + shifted(backs[1][k], "fsdp", -half - k).astype(f32)
    mix_first = spread_sum(outs[0])
    mix_first, (d_wide, grad_up, outs[1]) = together(mix_first, [d_wide, grad_up, outs[1]])

    d_h_two = d_wide[:, :D]
    share_e = d_wide[:, D : D + 2 * experts * F].reshape(T, experts, 2 * F).sum(axis=2)
    shares = jnp.sum(one_hot * share_e[:, None, :], axis=2)
    d_chosen = shares - weights * jnp.sum(shares, axis=1, keepdims=True)
    d_logits = jnp.sum(one_hot * d_chosen[:, :, None], axis=1).astype(bf16)
    d_h_two = d_h_two + contract_last(d_logits, wr_all)
    grad_router = contract_first(h_two, d_logits)

    d_out = out_grad[0].astype(f32)
    scaled_two = g_two * d_h_two
    d_resid = (
        d_out
        + r_two * scaled_two
        - resid * (r_two * r_two * r_two) * jnp.mean(resid * scaled_two, axis=1, keepdims=True)
    )
    grad_gain_two = jnp.sum(d_h_two * resid * r_two, axis=0)

    d_branch, grad_up = lax.optimization_barrier((row_major(d_resid.astype(bf16)), grad_up))
    d_branch = row_major(lax.all_gather(d_branch, "seq", axis=0, tiled=True))
    up_near = [sent(grad_up, k) for k in near]
    up_near, (d_branch, grad_up, outs[1]) = together(up_near, [d_branch, grad_up, outs[1]])
    up_back = dict(zip(near, up_near))
    up_far = [sent(grad_up, k) for k in far]
    d_att = contract_last(d_branch, wo_own).astype(bf16)
    grad_wo = contract_first(attended, d_branch).astype(bf16).reshape(F, sub, D)
    wo_back = return_heads(row_major(grad_wo), s, S, F)
    d_raw, d_sinks = attend_back(boundary, sinks, queries, kv, d_att, lse, cosine, sine)
    up_far, wo_back, (d_raw, outs[1]) = together(up_far, wo_back, [d_raw, outs[1]])
    up_back.update(zip(far, up_far))
    grad_wo = return_places(wo_back, s)
    wo_got = [sent(grad_wo, k) for k in range(1, F)]
    d_h_part, grad_gain_one = rows_back(d_raw, w_qkv, x_all, r_one_all)
    d_raw, d_h_part = lax.optimization_barrier((d_raw, d_h_part))
    d_h_one = lax.psum_scatter(d_h_part, "seq", scatter_dimension=0, tiled=True)
    grad_qkv = contract_first(h_one, d_raw).astype(bf16)
    grad_qkv = row_major(grad_qkv).reshape(F, rows_d, q_cols + 2 * head_dim)
    grad_expert_in = join_units(placed_parts(grad_gate, gate_back), placed_parts(grad_up, up_back), ff)[None]
    wo_got, (grad_qkv, outs[1], grad_expert_in) = together(wo_got, [grad_qkv, outs[1], grad_expert_in])
    qkv_got = [sent(grad_qkv, k) for k in range(1, F)]
    qkv_got[0], d_sinks, grad_gain_one, grad_gain_two, grad_router = lax.optimization_barrier(
        (qkv_got[0], d_sinks, grad_gain_one, grad_gain_two, grad_router)
    )
    qkv_got[0], *mix_first = lax.optimization_barrier((qkv_got[0], *mix_first))
    grad_wo = summed_parts(grad_wo, wo_got).astype(bf16)
    grad_output = row_major(lax.all_gather(row_major(grad_wo), "seq", axis=0, tiled=True)).astype(f32)
    mix_second = spread_sum(outs[1])
    mixed = sum(piece.astype(f32) for piece in mix_first).astype(bf16)
    mix_got = [shifted(mixed[k], "fsdp", -k) for k in range(1, half)]
    own_heads = jnp.zeros((heads,), f32)
    own_heads = lax.dynamic_update_slice_in_dim(own_heads, d_sinks[0, :heads_own], s * heads_own, 0)
    tiny = jnp.concatenate(
        [
            grad_gain_one[0].reshape(F, rows_d),
            grad_gain_two.reshape(F, rows_d),
            own_heads.reshape(F, own_sinks),
            grad_router.reshape(F, rows_d * experts),
        ],
        axis=1,
    )
    tiny = jnp.pad(tiny, ((0, 0), (0, round_up(cut[3], 16 * LANES) - cut[3]))).reshape(F, -1, LANES)
    tiny = sum_direct(tiny, "fsdp")
    d_h_one = d_h_one.astype(f32)
    r_one = lax.rsqrt(jnp.mean(x_f * x_f, axis=1, keepdims=True) + norm_eps)
    scaled_one = g_one * d_h_one
    input_grad = (
        d_resid
        + r_one * scaled_one
        - x_f * (r_one * r_one * r_one) * jnp.mean(x_f * scaled_one, axis=1, keepdims=True)
    )
    qkv_got, mix_second, mix_got, (input_grad, tiny, grad_output) = together(
        qkv_got, mix_second, mix_got, [input_grad, tiny, grad_output]
    )
    grad_qkv = summed_parts(grad_qkv, qkv_got).astype(bf16)
    grad_qkv = lax.all_gather(grad_qkv, "seq", axis=0)
    tiny = jnp.sum(gather_direct(tiny, "seq"), axis=0).reshape(-1)
    grad_query, grad_key, grad_value = join_heads(grad_qkv, q_cols, head_dim, kv_heads)

    mixture = mixed[0].astype(f32)
    mixed = sum(piece.astype(f32) for piece in mix_second).astype(bf16)
    for piece in mix_got + [shifted(mixed[k], "fsdp", -half - k) for k in range(half)]:
        mixture = mixture + piece.astype(f32)
    block_out = (resid + mixture[:, :D]).astype(bf16)

    return (
        block_out[None],
        input_grad[None],
        tiny[: cut[0]],
        grad_query,
        grad_key,
        grad_value,
        grad_output,
        tiny[cut[1] : cut[2]],
        tiny[cut[0] : cut[1]],
        tiny[cut[2] : cut[3]].reshape(rows_d, experts),
        grad_expert_in,
        grad_down[None],
    )


def solution(mesh):
    tokens = P("fsdp", "seq", None)
    vector = P("fsdp")
    matrix = P("fsdp", None)
    expert = P("seq", "fsdp", None)
    return jax.shard_map(
        local,
        mesh=mesh,
        in_specs=(
            tokens, tokens, vector, tokens, vector, matrix, matrix, matrix, matrix, vector, vector, matrix, expert, expert,
        ),
        out_specs=(
            tokens, tokens, vector, matrix, matrix, matrix, matrix, vector, vector, matrix, expert, expert,
        ),
        check_vma=False,
    )
```

```python
import functools

import jax
import jax.numpy as jnp
from jax import lax
from jax.experimental import pallas as pl
from jax.experimental.layout import Layout, with_layout_constraint
from jax.experimental.pallas import tpu as pltpu
from jax.sharding import PartitionSpec as P

WIN = 128
LANES = 128

norm_eps = 1e-05
theta_base = 150000.0
limit_value = 7.0
alpha_value = 1.702
score_scale = 0.125

f32 = jnp.float32
bf16 = jnp.bfloat16


def contract_last(left, right):
    return lax.dot_general(left, right, (((1,), (1,)), ((), ())), preferred_element_type=f32)


def contract_first(left, right):
    return lax.dot_general(left, right, (((0,), (0,)), ((), ())), preferred_element_type=f32)


def matmul(left, right):
    return jnp.dot(left, right, preferred_element_type=f32)


def round_up(value, unit):
    return -(-value // unit) * unit


def partner(values):
    lane = lax.broadcasted_iota(jnp.int32, values.shape, 1)
    return jnp.where(lane % 64 < 32, pltpu.roll(values, 96, 1), pltpu.roll(values, 32, 1))


def allowed_keys(block, split_at):
    row = lax.broadcasted_iota(jnp.int32, (WIN, 2 * WIN), 0) + block * WIN
    key = lax.broadcasted_iota(jnp.int32, (WIN, 2 * WIN), 1) + (block - 1) * WIN
    distance = row - key
    return (
        (distance >= 0)
        & (distance < WIN)
        & (key >= 0)
        & ((row >= split_at) == (key >= split_at))
    )


def both_halves(keys_values, low):
    lane = lax.broadcasted_iota(jnp.int32, keys_values.shape, 1)
    other = pltpu.roll(keys_values, 64, 1)
    return jnp.where((lane < 64) == low, keys_values, other)


def attend_kernel(split_ref, sink_ref, qkv_ref, cos_ref, sin_ref, q_ref, kv_ref, att_ref, lse_ref):
    tokens = qkv_ref.shape[0]
    width = q_ref.shape[1]
    pairs = width // LANES
    split_at = split_ref[0]
    lane = lax.broadcasted_iota(jnp.int32, (WIN, LANES), 1)

    def body(block, carry):
        rows = pl.ds(pl.multiple_of(block * WIN, WIN), WIN)
        back = pl.ds(pl.multiple_of(jnp.maximum(block - 1, 0) * WIN, WIN), WIN)
        cosine = cos_ref[rows, :]
        sine = sin_ref[rows, :]
        kv_raw = qkv_ref[rows, width:]
        kv_now = jnp.where(lane < 64, kv_raw * cosine + partner(kv_raw) * sine, kv_raw)
        kv_ref[rows, :] = kv_now.astype(bf16)
        kv_two = jnp.concatenate([kv_ref[back, :].astype(f32), kv_now.astype(bf16).astype(f32)], axis=0)
        keys = both_halves(kv_two, True).astype(bf16)
        values = both_halves(kv_two, False).astype(bf16)
        allowed = allowed_keys(block, split_at)
        stats = jnp.zeros((WIN, LANES), f32)
        for pair in range(pairs):
            at = pl.ds(pair * LANES, LANES)
            raw = qkv_ref[rows, at]
            turned = (raw * cosine + partner(raw) * sine).astype(bf16)
            q_ref[rows, at] = turned
            outs = []
            for half in range(2):
                head = 2 * pair + half
                picked = jnp.where((lane < 64) == (half == 0), turned.astype(f32), 0.0).astype(bf16)
                scores = contract_last(picked, keys) * score_scale
                masked = jnp.where(allowed, scores, -1e30)
                sink = sink_ref[head]
                top = jnp.maximum(jnp.max(masked, axis=1, keepdims=True), sink)
                exps = jnp.where(allowed, jnp.exp(masked - top), 0.0)
                denom = jnp.sum(exps, axis=1, keepdims=True) + jnp.exp(sink - top)
                probs = (exps * (1.0 / denom)).astype(bf16)
                outs.append(matmul(probs, values))
                stats = jnp.where(lane == head, top + jnp.log(denom), stats)
            att_ref[rows, at] = jnp.where(lane < 64, outs[0], outs[1]).astype(bf16)
        lse_ref[rows, :] = stats
        return carry

    lax.fori_loop(0, tokens // WIN, body, 0)


def attend(split_at, sinks, qkv, cosine, sine, width):
    tokens = qkv.shape[0]
    vmem = pl.BlockSpec(memory_space=pltpu.VMEM)
    smem = pl.BlockSpec(memory_space=pltpu.SMEM)
    return pl.pallas_call(
        attend_kernel,
        out_shape=(
            jax.ShapeDtypeStruct((tokens, width), bf16),
            jax.ShapeDtypeStruct((tokens, LANES), bf16),
            jax.ShapeDtypeStruct((tokens, width), bf16),
            jax.ShapeDtypeStruct((tokens, LANES), f32),
        ),
        in_specs=[smem, smem, vmem, vmem, vmem],
        out_specs=(vmem, vmem, vmem, vmem),
        compiler_params=pltpu.CompilerParams(vmem_limit_bytes=32 * 2**20),
        cost_estimate=pl.CostEstimate(
            flops=tokens * width * 2 * WIN * 8, bytes_accessed=8 * 2**20, transcendentals=0
        ),
        name="attend",
    )(split_at, sinks, qkv, cosine, sine)


def attend_back_kernel(
    split_ref, sink_ref, q_ref, kv_ref, datt_ref, lse_ref, cos_ref, sin_ref, draw_ref, dsink_ref, dk_acc, dv_acc
):
    tokens = q_ref.shape[0]
    width = q_ref.shape[1]
    pairs = width // LANES
    split_at = split_ref[0]
    lane = lax.broadcasted_iota(jnp.int32, (WIN, LANES), 1)
    lane_row = lax.broadcasted_iota(jnp.int32, (8, LANES), 1)
    dk_acc[...] = jnp.zeros_like(dk_acc)
    dv_acc[...] = jnp.zeros_like(dv_acc)

    def body(block, sink_sum):
        rows = pl.ds(pl.multiple_of(block * WIN, WIN), WIN)
        back = pl.ds(pl.multiple_of(jnp.maximum(block - 1, 0) * WIN, WIN), WIN)
        both = pl.ds(pl.multiple_of(block * WIN, WIN), 2 * WIN)
        cosine = cos_ref[rows, :]
        sine = sin_ref[rows, :]
        kv_two = jnp.concatenate([kv_ref[back, :], kv_ref[rows, :]], axis=0).astype(f32)
        keys = both_halves(kv_two, True).astype(bf16)
        values = both_halves(kv_two, False).astype(bf16)
        allowed = allowed_keys(block, split_at)
        stats = lse_ref[rows, :]
        d_keys = jnp.zeros((2 * WIN, LANES), f32)
        d_values = jnp.zeros((2 * WIN, LANES), f32)
        for pair in range(pairs):
            at = pl.ds(pair * LANES, LANES)
            turned = q_ref[rows, at].astype(f32)
            d_out = datt_ref[rows, at].astype(f32)
            d_turned = []
            for half in range(2):
                head = 2 * pair + half
                mine = (lane < 64) == (half == 0)
                picked = jnp.where(mine, turned, 0.0).astype(bf16)
                d_picked = jnp.where(mine, d_out, 0.0).astype(bf16)
                total = stats[:, head : head + 1]
                scores = contract_last(picked, keys) * score_scale
                probs = jnp.where(allowed, jnp.exp(scores - total), 0.0)
                d_probs = contract_last(d_picked, values)
                delta = jnp.sum(probs * d_probs, axis=1, keepdims=True)
                d_scores = (probs * (d_probs - delta)).astype(bf16)
                share = jnp.sum(jnp.exp(sink_ref[head] - total) * delta)
                sink_sum = sink_sum - jnp.where(lane_row == head, share, 0.0)
                d_turned.append(matmul(d_scores, keys))
                d_keys = d_keys + contract_first(d_scores, picked)
                d_values = d_values + contract_first(probs.astype(bf16), d_picked)
            d_query = jnp.where(lane < 64, d_turned[0], d_turned[1]) * score_scale
            draw_ref[rows, at] = (d_query * cosine - partner(d_query) * sine).astype(bf16)
        dk_acc[both, :] += d_keys
        dv_acc[both, :] += d_values
        return sink_sum

    dsink_ref[...] = lax.fori_loop(0, tokens // WIN, body, jnp.zeros((8, LANES), f32))

    def finish(block, carry):
        rows = pl.ds(pl.multiple_of(block * WIN, WIN), WIN)
        held = pl.ds(pl.multiple_of((block + 1) * WIN, WIN), WIN)
        d_keys = dk_acc[held, :]
        d_keys = (d_keys + pltpu.roll(d_keys, 64, 1)) * score_scale
        d_keys = d_keys * cos_ref[rows, :] - partner(d_keys) * sin_ref[rows, :]
        d_values = dv_acc[held, :]
        d_values = d_values + pltpu.roll(d_values, 64, 1)
        draw_ref[rows, width:] = jnp.where(lane < 64, d_keys, d_values).astype(bf16)
        return carry

    lax.fori_loop(0, tokens // WIN, finish, 0)


def attend_back(split_at, sinks, queries, kv, d_att, lse, cosine, sine):
    tokens, width = queries.shape
    vmem = pl.BlockSpec(memory_space=pltpu.VMEM)
    smem = pl.BlockSpec(memory_space=pltpu.SMEM)
    return pl.pallas_call(
        attend_back_kernel,
        out_shape=(
            jax.ShapeDtypeStruct((tokens, width + LANES), bf16),
            jax.ShapeDtypeStruct((8, LANES), f32),
        ),
        in_specs=[smem, smem, vmem, vmem, vmem, vmem, vmem, vmem],
        out_specs=(vmem, vmem),
        scratch_shapes=[pltpu.VMEM((tokens + WIN, LANES), f32), pltpu.VMEM((tokens + WIN, LANES), f32)],
        compiler_params=pltpu.CompilerParams(vmem_limit_bytes=32 * 2**20),
        cost_estimate=pl.CostEstimate(
            flops=tokens * width * 2 * WIN * 20, bytes_accessed=8 * 2**20, transcendentals=0
        ),
        name="attend_back",
    )(split_at, sinks, queries, kv, d_att, lse, cosine, sine)


def expert_kernel(units, first, *refs):
    experts, capacity, tile = units
    ids_ref, h_ref, g_ref, wg_ref, wu_ref, wd_ref = refs[:6]
    refs = refs[6:] if first else refs[10:]
    back_ref, own_ref, other_ref, x_ref, gr_ref, act_ref, du_ref, xf, gf = refs
    parity = ids_ref[2]
    T = h_ref.shape[2]
    D = wd_ref.shape[1]
    ffp = wd_ref.shape[0]
    at_blocks = [(i, j) for i in range(h_ref.shape[0]) for j in range(h_ref.shape[1])]
    expert = ids_ref[0]
    place_col = ids_ref[1]
    tail = h_ref.shape[3] - LANES
    base = D - tail
    lane = lax.broadcasted_iota(jnp.int32, (T, LANES), 1)
    row = lax.broadcasted_iota(jnp.int32, (T, T), 0)
    col = lax.broadcasted_iota(jnp.int32, (T, T), 1)
    before = jnp.where(col < row, 1.0, 0.0).astype(bf16)
    places = []
    weights = []
    for b, (i, j) in enumerate(at_blocks):
        last = h_ref[i, j, :, tail:].astype(f32)
        hit = jnp.sum(jnp.where(lane == base + 3 * experts + expert, last, 0.0), axis=1, keepdims=True)
        hits = jnp.broadcast_to(hit, (T, LANES))
        slot = matmul(before, hits.astype(bf16))
        place = jnp.where((slot == lane.astype(f32)) & (hits > 0.5), 1.0, 0.0)[:, :capacity].astype(bf16)
        places.append(place)
        at = pl.ds(b * capacity, capacity)
        xf[at, :] = contract_first(place, h_ref[i, j])
        ends = xf[at, tail:]
        lane_c = lax.broadcasted_iota(jnp.int32, ends.shape, 1) - base - expert
        mine = (lane_c == 0) | (lane_c == experts) | (lane_c == 2 * experts)
        weight = jnp.sum(jnp.where(mine, ends, 0.0), axis=1, keepdims=True)
        weights.append(weight)
        gf[at, :] = contract_first(place, g_ref[i, j]) * weight
    x_ref[...] = xf[:, :D].astype(bf16)
    gr_ref[...] = gf[:, :D].astype(bf16)
    weight_all = jnp.concatenate(weights, axis=0)
    share = jnp.zeros_like(weight_all)
    for n in range(ffp // tile):
        at = pl.ds(n * tile, tile)
        at_up = pl.ds(ffp + n * tile, tile)
        gate = matmul(x_ref[...], wg_ref[:, at])
        up = matmul(x_ref[...], wu_ref[:, at])
        d_act = contract_last(gr_ref[...], wd_ref[at, :])
        clipped = jnp.minimum(gate, limit_value)
        up_one = jnp.clip(up, -limit_value, limit_value) + 1.0
        sig = 1.0 / (1.0 + jnp.exp(-alpha_value * clipped))
        swish = clipped * sig
        act = (up_one * swish).astype(bf16)
        act_ref[:, at] = act
        share = share + jnp.sum(act.astype(f32) * d_act, axis=1, keepdims=True)
        d_gate = jnp.where(
            gate < limit_value, d_act * up_one * (sig + alpha_value * swish * (1.0 - sig)), 0.0
        )
        d_up = jnp.where((up > -limit_value) & (up < limit_value), d_act * swish, 0.0)
        du_ref[:, at] = d_gate.astype(bf16)
        du_ref[:, at_up] = d_up.astype(bf16)
    step = 1536
    for start in range(0, D, step):
        size = min(step, D - start)
        d_rows = contract_last(du_ref[:, :ffp], wg_ref[start : start + size, :])
        d_rows = d_rows + contract_last(du_ref[:, ffp:], wu_ref[start : start + size, :])
        for b, (i, j) in enumerate(at_blocks):
            part = d_rows[b * capacity : (b + 1) * capacity].astype(bf16)
            back_ref[i, j, :, start : start + size] = matmul(places[b], part).astype(bf16)
    high = share.astype(bf16).astype(f32)
    spare = back_ref.shape[3] - D
    lane_s = lax.broadcasted_iota(jnp.int32, (capacity, spare), 1)
    for b, (i, j) in enumerate(at_blocks):
        own = slice(b * capacity, (b + 1) * capacity)
        terms = jnp.where(lane_s == place_col, high[own], 0.0)
        terms = jnp.where(lane_s == place_col + 1, share[own] - high[own], terms)
        back_ref[i, j, :, D:] = matmul(places[b], terms.astype(bf16)).astype(bf16)
    groups = h_ref.shape[1]
    if own_ref.shape[3] > D:
        own_ref[0, :, :, D:] = jnp.zeros((groups, T, own_ref.shape[3] - D), bf16)
        other_ref[0, :, :, D:] = jnp.zeros((groups, T, own_ref.shape[3] - D), bf16)
    for start in range(0, D, step):
        size = min(step, D - start)
        rows = matmul(act_ref[...], wd_ref[:, start : start + size]) * weight_all
        for j in range(groups):
            pair = []
            for b in (j, groups + j):
                part = rows[b * capacity : (b + 1) * capacity].astype(bf16)
                pair.append(matmul(places[b], part))
            own_ref[0, j, :, start : start + size] = jnp.where(parity == 0, pair[0], pair[1]).astype(bf16)
            other_ref[0, j, :, start : start + size] = jnp.where(parity == 0, pair[1], pair[0]).astype(bf16)


def run_expert(ids, h_part, g_all, w_gate, w_up, w_down, experts, capacity, spare, half, kept):
    S, FH, T, wide = h_part.shape
    ffp, D = w_down.shape
    lead, deep = 2, min(FH, 2)
    grid = (S // lead, FH // deep)
    tile = 256 if ffp % 256 == 0 else LANES
    rows = lead * deep * capacity
    smem = pl.BlockSpec(memory_space=pltpu.SMEM)
    held = pl.BlockSpec(memory_space=pl.ANY)
    before = half * grid[1]

    def tokens(width, skip=0):
        return pl.BlockSpec((lead, deep, T, width), lambda i, j: (i, j + skip, 0, 0))

    pair = pl.BlockSpec((1, deep, T, wide), lambda i, j: (i, j, 0, 0))

    def slots(width):
        return pl.BlockSpec((rows, width), lambda i, j: ((half * grid[0] + i) * grid[1] + j, 0))

    def whole(shape):
        return pl.BlockSpec(shape, lambda i, j: (0, 0), pipeline_mode=pl.Buffered(1))

    total = 2 * S * FH * capacity
    first = kept is None
    extra = () if first else tuple(kept)
    return pl.pallas_call(
        functools.partial(expert_kernel, (experts, capacity, tile), first),
        grid=grid,
        out_shape=(
            jax.ShapeDtypeStruct((S, FH, T, D + spare), bf16),
            jax.ShapeDtypeStruct((S // 2, FH, T, wide), bf16),
            jax.ShapeDtypeStruct((S // 2, FH, T, wide), bf16),
            jax.ShapeDtypeStruct((total, D), bf16),
            jax.ShapeDtypeStruct((total, D), bf16),
            jax.ShapeDtypeStruct((total, ffp), bf16),
            jax.ShapeDtypeStruct((total, 2 * ffp), bf16),
        ),
        in_specs=[smem, tokens(wide), tokens(wide, before)]
        + [whole(w.shape) for w in (w_gate, w_up, w_down)]
        + [held] * len(extra),
        out_specs=(tokens(D + spare), pair, pair, slots(D), slots(D), slots(ffp), slots(2 * ffp)),
        input_output_aliases={6 + k: 3 + k for k in range(len(extra))},
        scratch_shapes=[pltpu.VMEM((rows, wide), f32)] * 2,
        compiler_params=pltpu.CompilerParams(vmem_limit_bytes=62 * 2**20),
        cost_estimate=pl.CostEstimate(
            flops=total * D * ffp * 6, bytes_accessed=60 * 2**20, transcendentals=0
        ),
        name="experts",
    )(ids, h_part, g_all, w_gate, w_up, w_down, *extra)


def rows_at_once(rows):
    return 144 if rows % 144 == 0 else rows


def cut_kernel(parts, ff, w_ref, gate_ref, up_ref):
    for half, out_ref in enumerate((gate_ref, up_ref)):
        ffp = out_ref.shape[2]
        for part in range(parts):
            first = (half * parts + part) * ff
            out_ref[part, :, :ff] = w_ref[:, first : first + ff]
            if ffp > ff:
                out_ref[part, :, ff:] = jnp.zeros((w_ref.shape[0], ffp - ff), bf16)


def cut_units(w, parts, ff, ffp):
    rows = w.shape[0]
    step = rows_at_once(rows)
    return pl.pallas_call(
        functools.partial(cut_kernel, parts, ff),
        grid=(rows // step,),
        out_shape=(jax.ShapeDtypeStruct((parts, rows, ffp), bf16),) * 2,
        in_specs=[pl.BlockSpec((step, w.shape[1]), lambda i: (i, 0))],
        out_specs=(pl.BlockSpec((parts, step, ffp), lambda i: (0, i, 0)),) * 2,
        compiler_params=pltpu.CompilerParams(vmem_limit_bytes=40 * 2**20),
        cost_estimate=pl.CostEstimate(flops=0, bytes_accessed=4 * w.size, transcendentals=0),
        name="cut_units",
    )(w)


def join_kernel(ff, gate_ref, up_ref, out_ref):
    for half, g_ref in enumerate((gate_ref, up_ref)):
        parts = g_ref.shape[0]
        for part in range(parts):
            first = (half * parts + part) * ff
            out_ref[:, first : first + ff] = g_ref[part, :, :ff].astype(f32)


def join_units(gate, up, ff):
    parts, rows, width = gate.shape
    step = rows_at_once(rows)
    return pl.pallas_call(
        functools.partial(join_kernel, ff),
        grid=(rows // step,),
        out_shape=jax.ShapeDtypeStruct((rows, 2 * parts * ff), f32),
        in_specs=[pl.BlockSpec((parts, step, width), lambda i: (0, i, 0))] * 2,
        out_specs=pl.BlockSpec((step, 2 * parts * ff), lambda i: (i, 0)),
        compiler_params=pltpu.CompilerParams(vmem_limit_bytes=48 * 2**20),
        cost_estimate=pl.CostEstimate(flops=0, bytes_accessed=12 * gate.size, transcendentals=0),
        name="join_units",
    )(gate, up)


def heads_kernel(q_cols, head_dim, g_ref, q_ref, k_ref, v_ref):
    sources = g_ref.shape[0]
    kv_heads = k_ref.shape[1] // head_dim
    repeat = sources // kv_heads
    for source in range(sources):
        q_ref[:, source * q_cols : (source + 1) * q_cols] = g_ref[source, :, :q_cols].astype(f32)
    for out_ref, begin in ((k_ref, q_cols), (v_ref, q_cols + head_dim)):
        for head in range(kv_heads):
            total = g_ref[head * repeat, :, begin : begin + head_dim].astype(f32)
            for other in range(1, repeat):
                total = total + g_ref[head * repeat + other, :, begin : begin + head_dim].astype(f32)
            out_ref[:, head * head_dim : (head + 1) * head_dim] = total


def join_heads(grads, q_cols, head_dim, kv_heads):
    sources, rows, width = grads.shape
    step = rows_at_once(rows)
    kv_cols = kv_heads * head_dim
    return pl.pallas_call(
        functools.partial(heads_kernel, q_cols, head_dim),
        grid=(rows // step,),
        out_shape=(
            jax.ShapeDtypeStruct((rows, sources * q_cols), f32),
            jax.ShapeDtypeStruct((rows, kv_cols), f32),
            jax.ShapeDtypeStruct((rows, kv_cols), f32),
        ),
        in_specs=[pl.BlockSpec((sources, step, width), lambda i: (0, i, 0))],
        out_specs=(
            pl.BlockSpec((step, sources * q_cols), lambda i: (i, 0)),
            pl.BlockSpec((step, kv_cols), lambda i: (i, 0)),
            pl.BlockSpec((step, kv_cols), lambda i: (i, 0)),
        ),
        compiler_params=pltpu.CompilerParams(vmem_limit_bytes=48 * 2**20),
        cost_estimate=pl.CostEstimate(flops=0, bytes_accessed=6 * grads.size, transcendentals=0),
        name="join_heads",
    )(grads)


def gather_direct(value, axis):
    count = lax.axis_size(axis)
    spread = jnp.broadcast_to(value[None], (count,) + value.shape)
    return lax.all_to_all(spread, axis, split_axis=0, concat_axis=0, tiled=True)


def sum_direct(parts, axis):
    got = lax.all_to_all(parts, axis, split_axis=0, concat_axis=0, tiled=True)
    return jnp.sum(got.astype(f32), axis=0)


def shifted(value, axis, steps):
    count = lax.axis_size(axis)
    return lax.ppermute(value, axis, [(i, (i + steps) % count) for i in range(count)])


def taken(parts, index):
    return lax.dynamic_index_in_dim(parts, index, 0, keepdims=False)


def sent(parts, k):
    count = lax.axis_size("fsdp")
    return shifted(taken(parts, (lax.axis_index("fsdp") + k) % count), "fsdp", k)


def placed_parts(parts, got):
    count = lax.axis_size("fsdp")
    for k, piece in got.items():
        parts = lax.dynamic_update_index_in_dim(
            parts, piece, (lax.axis_index("fsdp") - k) % count, 0
        )
    return parts


def summed_parts(parts, got):
    total = taken(parts, lax.axis_index("fsdp")).astype(f32)
    for piece in got:
        total = total + piece.astype(f32)
    return total


def sum_turned(parts, axis):
    total = parts[0].astype(f32)
    for k in range(1, len(parts)):
        total = total + shifted(parts[k], axis, -k).astype(f32)
    return total


def row_major(value):
    return with_layout_constraint(value, Layout(major_to_minor=tuple(range(value.ndim))))


def after(value, *others):
    return lax.optimization_barrier((value,) + others)[0]


def together(*lists):
    flat = lax.optimization_barrier(tuple(item for items in lists for item in items))
    result, at = [], 0
    for items in lists:
        result.append(list(flat[at : at + len(items)]))
        at += len(items)
    return result


def flat_tiles(items, dtype):
    flat = jnp.concatenate([item.reshape(-1) for item in items]).astype(dtype)
    padded = round_up(flat.shape[0], 16 * LANES)
    return jnp.pad(flat, (0, padded - flat.shape[0])).reshape(-1, LANES)


def back_kernel(d_ref, w_ref, x_ref, r_ref, out_ref, gain_ref):
    d_h = contract_last(d_ref[...], w_ref[...])
    out_ref[...] = d_h.astype(bf16)
    sums = jnp.sum(d_h * x_ref[...].astype(f32) * r_ref[...], axis=0, keepdims=True)

    @pl.when(pl.program_id(0) == 0)
    def _():
        gain_ref[...] = jnp.zeros_like(gain_ref)

    gain_ref[...] += jnp.broadcast_to(sums, gain_ref.shape)


def rows_back(d_raw, w_qkv, x_all, r_all):
    rows, width = d_raw.shape
    D = w_qkv.shape[0]
    step = 256
    return pl.pallas_call(
        back_kernel,
        grid=(rows // step,),
        out_shape=(jax.ShapeDtypeStruct((rows, D), bf16), jax.ShapeDtypeStruct((8, D), f32)),
        in_specs=[
            pl.BlockSpec((step, width), lambda i: (i, 0)),
            pl.BlockSpec((D, width), lambda i: (0, 0)),
            pl.BlockSpec((step, D), lambda i: (i, 0)),
            pl.BlockSpec((step, 1), lambda i: (i, 0)),
        ],
        out_specs=(pl.BlockSpec((step, D), lambda i: (i, 0)), pl.BlockSpec((8, D), lambda i: (0, 0))),
        compiler_params=pltpu.CompilerParams(vmem_limit_bytes=40 * 2**20),
        cost_estimate=pl.CostEstimate(
            flops=2 * rows * D * width, bytes_accessed=20 * 2**20, transcendentals=0
        ),
        name="rows_back",
    )(d_raw, w_qkv, x_all, r_all)


def spread_tables(S, F):
    ratio = S // F
    return [[(src, ((src + k) % F) * ratio + src // F) for src in range(S)] for k in range(F)]


def gather_heads(pieces, s, S, F):
    ratio = S // F
    rows = jnp.zeros_like(pieces)
    for k, perm in enumerate(spread_tables(S, F)):
        sent = lax.dynamic_index_in_dim(pieces, (s + k) % F, 0, keepdims=False)
        got = lax.ppermute(sent, "seq", perm)
        rows = lax.dynamic_update_index_in_dim(rows, got, (s // ratio - k) % F, 0)
    return rows


def return_heads(rows, s, S, F):
    ratio = S // F
    got = []
    for k, perm in enumerate(spread_tables(S, F)):
        sent = lax.dynamic_index_in_dim(rows, (s // ratio - k) % F, 0, keepdims=False)
        got.append(lax.ppermute(sent, "seq", [(b, a) for a, b in perm]))
    return got


def return_places(got, s):
    pieces = jnp.broadcast_to(got[0][None], (len(got),) + got[0].shape)
    for k, piece in enumerate(got):
        pieces = lax.dynamic_update_index_in_dim(pieces, piece, (s + k) % len(got), 0)
    return pieces


def local(
    hidden_in,
    out_grad,
    boundary,
    routes,
    gain_one,
    w_query,
    w_key,
    w_value,
    w_output,
    sink_logits,
    gain_two,
    w_router,
    w_in,
    w_out,
):
    S = lax.axis_size("seq")
    F = lax.axis_size("fsdp")
    s = lax.axis_index("seq")
    z = lax.axis_index("fsdp")
    T, D = hidden_in.shape[1:]
    Tg = S * T
    rows_d = w_query.shape[0]
    heads = sink_logits.shape[0] * F
    head_dim = w_query.shape[1] // heads
    kv_heads = w_key.shape[1] // head_dim
    group_size = heads // kv_heads
    heads_own = heads // S
    q_cols = heads_own * head_dim
    experts = w_router.shape[1]
    top_count = routes.shape[2]
    capacity = T * top_count * 9 // (8 * experts)
    ff = w_out.shape[1]
    ffp = round_up(ff, LANES)
    sub = w_output.shape[0] // S
    ratio = S // F

    x_own = hidden_in[0]
    x_all = row_major(lax.all_gather(row_major(x_own), "seq", axis=0, tiled=True))

    kv_head = (s * heads_own) // group_size
    qkv_shard = jnp.concatenate(
        [
            lax.dynamic_slice_in_dim(w_query, s * q_cols, q_cols, 1),
            lax.dynamic_slice_in_dim(w_key, kv_head * head_dim, head_dim, 1),
            lax.dynamic_slice_in_dim(w_value, kv_head * head_dim, head_dim, 1),
        ],
        axis=1,
    )
    w_qkv = lax.all_gather(after(qkv_shard, x_all), "fsdp", axis=0, tiled=True)

    small = flat_tiles((gain_one, gain_two, sink_logits, w_router), bf16)
    small_all = gather_direct(small, "fsdp").reshape(F, -1)
    own_sinks = sink_logits.shape[0]
    cut = [rows_d, 2 * rows_d, 2 * rows_d + own_sinks, 2 * rows_d + own_sinks + rows_d * experts]
    g_one = small_all[:, : cut[0]].reshape(1, D).astype(f32)
    g_two = small_all[:, cut[0] : cut[1]].reshape(1, D).astype(f32)
    sink_all = small_all[:, cut[1] : cut[2]].reshape(heads).astype(f32)
    wr_all = small_all[:, cut[2] : cut[3]].reshape(D, experts)
    sinks = lax.dynamic_slice_in_dim(sink_all, s * heads_own, heads_own, 0)

    split_at = boundary[0]
    token = jnp.arange(Tg, dtype=jnp.int32)
    positions = token - jnp.where(token >= split_at, split_at, 0)
    half_dim = head_dim // 2
    frequency = jnp.exp(-jnp.log(theta_base) * (2.0 * jnp.arange(half_dim, dtype=f32)) / head_dim)
    angles = positions.astype(f32)[:, None] * frequency[None, :]
    cos_half, sin_half = jnp.cos(angles), jnp.sin(angles)
    cosine = jnp.concatenate([cos_half] * 4, axis=1)
    sine = jnp.concatenate([-sin_half, sin_half] * 2, axis=1)

    x_all_f = x_all.astype(f32)
    r_one_all = lax.rsqrt(jnp.mean(x_all_f * x_all_f, axis=1, keepdims=True) + norm_eps)
    h_one = (x_all_f * r_one_all * g_one).astype(bf16)
    wo_sub = lax.dynamic_slice_in_dim(w_output, s * sub, sub, 0)
    wo_pieces = jnp.broadcast_to(wo_sub[None], (F, sub, D))
    for k in range(1, F):
        wo_pieces = lax.dynamic_update_index_in_dim(
            wo_pieces, shifted(wo_sub, "fsdp", k), (z - k) % F, 0
        )
    wo_own = gather_heads(wo_pieces, s, S, F).reshape(F * sub, D)

    half = F // 2
    wide = round_up(D + 4 * experts, LANES)
    near = [1, F - 1]
    far = [k for k in range(1, F) if k not in near]
    d_own = jnp.pad(out_grad[0], ((0, 0), (0, wide - D)))
    cut_gate, cut_up = cut_units(w_in[0], F, ff, ffp)
    w_down = jnp.pad(w_out[0], ((0, ffp - ff), (0, 0)))
    d_own, cut_gate, cut_up, w_down, w_qkv = lax.optimization_barrier(
        (d_own, cut_gate, cut_up, w_down, w_qkv)
    )
    qkv = matmul(h_one, w_qkv)
    queries, kv, attended, lse = attend(boundary, sinks, qkv, cosine, sine, q_cols)
    d_out_got = {k: shifted(d_own, "fsdp", k) for k in near}

    branch_part = row_major(matmul(attended, wo_own).astype(bf16))
    (branch_part, d_own, cut_gate), near_got = together(
        [branch_part, d_own, cut_gate], [d_out_got[k] for k in near]
    )
    d_out_got = dict(zip(near, near_got))
    branch = lax.psum_scatter(branch_part, "seq", scatter_dimension=0, tiled=True)
    far_got = [shifted(d_own, "fsdp", k) for k in far]
    gate_got = {near[0]: sent(cut_gate, near[0])}
    (branch, gate_got[near[0]]), far_got = together([branch, gate_got[near[0]]], far_got)
    d_out_got.update(zip(far, far_got))
    d_stack = row_major(jnp.stack([d_own] + [d_out_got[k] for k in range(1, F)]))

    def over_seq(stack):
        return row_major(lax.all_gather(stack, "seq", axis=0))

    d_out_all = over_seq(d_stack)
    x_f = x_own.astype(f32)
    resid = x_f + branch.astype(f32)
    r_two = lax.rsqrt(jnp.mean(resid * resid, axis=1, keepdims=True) + norm_eps)
    h_two = (resid * r_two * g_two).astype(bf16)

    blocks = S * F
    one_hot = (routes[0][:, :, None] == jnp.arange(experts, dtype=jnp.int32)).astype(f32)
    logits = matmul(h_two, wr_all)
    chosen = jnp.sum(one_hot * logits[:, None, :], axis=2)
    weights = jax.nn.softmax(chosen, axis=1)
    weight_e = jnp.sum(one_hot * weights[:, :, None], axis=1)
    hit_e = jnp.sum(one_hot, axis=1)
    high = lax.reduce_precision(weight_e, 8, 7)
    middle = lax.reduce_precision(weight_e - high, 8, 7)
    low = weight_e - high - middle
    fill = jnp.zeros((T, wide - D - 4 * experts), bf16)
    h_two_wide = jnp.concatenate(
        [h_two] + [part.astype(bf16) for part in (high, middle, low, hit_e)] + [fill], axis=1
    )

    h_two_wide, d_stack, cut_gate = lax.optimization_barrier((h_two_wide, d_stack, cut_gate))
    h_two_got = [shifted(h_two_wide, "fsdp", k) for k in range(1, F)]
    gate_far = [sent(cut_gate, k) for k in far]
    h_two_got, gate_far, (cut_gate, cut_up) = together(h_two_got, gate_far, [cut_gate, cut_up])
    h_turned = [h_two_wide] + h_two_got
    h_near = row_major(jnp.stack(h_turned[:half]))
    h_far = row_major(jnp.stack(h_turned[half:]))
    h_near, d_out_all = lax.optimization_barrier((h_near, d_out_all))
    h_parts = [over_seq(h_near)]
    gate_got.update(zip(far, gate_far))
    gate_last, up_first = sent(cut_gate, near[1]), sent(cut_up, near[0])
    gate_last, up_first, h_far, cut_up = lax.optimization_barrier((gate_last, up_first, h_far, cut_up))
    h_parts.append(over_seq(h_far))
    gate_got[near[1]] = gate_last
    up_got = {near[0]: up_first}
    up_got.update({k: sent(cut_up, k) for k in range(1, F) if k not in up_got})
    w_gate = placed_parts(cut_gate, gate_got).reshape(D, ffp)
    w_up = placed_parts(cut_up, up_got).reshape(D, ffp)

    spare = round_up(D + 2 * experts * F, LANES) - D
    ids = jnp.stack([s, 2 * (s * F + z), s % 2])
    def to_group(parts):
        return row_major(lax.psum_scatter(parts, "seq", scatter_dimension=0, tiled=True))[0]

    def swapped(parts):
        return lax.ppermute(parts, "seq", [(i, i ^ 1) for i in range(S)])

    def added(left, right):
        return (left.astype(f32) + right.astype(f32)).astype(bf16)

    def spread_sum(parts):
        pairs = S // 2
        own = taken(parts, s // 2)
        return [own] + [shifted(taken(parts, (s // 2 + k) % pairs), "seq", 2 * k) for k in range(1, pairs)]

    args = (w_gate, w_up, w_down, experts, capacity, spare)
    back, mine, other, *kept = run_expert(ids, h_parts[0], d_out_all, *args, 0, None)
    backs = [to_group(back)]
    back, mine_two, other_two, *kept = run_expert(ids, h_parts[1], d_out_all, *args, 1, kept)
    backs.append(to_group(back))
    rows_x, rows_g, activation, d_units = kept
    other, other_two = swapped(row_major(other)), swapped(row_major(other_two))

    def units_grad(units):
        grad = contract_first(rows_x, units).astype(bf16)
        return row_major(grad).reshape(F, rows_d, ffp)

    grad_gate = units_grad(d_units[:, :ffp])
    gate_first = sent(grad_gate, near[0])
    d_units, gate_first, grad_gate, backs[0], other, other_two = lax.optimization_barrier(
        (d_units, gate_first, grad_gate, backs[0], other, other_two)
    )
    outs = [row_major(added(mine, other)), row_major(added(mine_two, other_two))]
    grad_up = units_grad(d_units[:, ffp:])
    gate_rest = [sent(grad_gate, k) for k in near[1:] + far]
    back_near = [shifted(backs[0][k], "fsdp", -k) for k in range(1, half)]
    grad_down = contract_first(activation, rows_g)[:ff]
    (backs[1], grad_up, grad_down), gate_rest, back_near, outs = together(
        [backs[1], grad_up, grad_down], gate_rest, back_near, outs
    )
    gate_back = dict(zip(near + far, [gate_first] + gate_rest))
    d_wide = backs[0][0].astype(f32)
    for piece in back_near:
        d_wide = d_wide + piece.astype(f32)
    for k in range(half):
        d_wide = d_wide + shifted(backs[1][k], "fsdp", -half - k).astype(f32)
    mix_first = spread_sum(outs[0])
    mix_first, (d_wide, grad_up, outs[1]) = together(mix_first, [d_wide, grad_up, outs[1]])

    d_h_two = d_wide[:, :D]
    share_e = d_wide[:, D : D + 2 * experts * F].reshape(T, experts, 2 * F).sum(axis=2)
    shares = jnp.sum(one_hot * share_e[:, None, :], axis=2)
    d_chosen = shares - weights * jnp.sum(shares, axis=1, keepdims=True)
    d_logits = jnp.sum(one_hot * d_chosen[:, :, None], axis=1).astype(bf16)
    d_h_two = d_h_two + contract_last(d_logits, wr_all)
    grad_router = contract_first(h_two, d_logits)

    d_out = out_grad[0].astype(f32)
    scaled_two = g_two * d_h_two
    d_resid = (
        d_out
        + r_two * scaled_two
        - resid * (r_two * r_two * r_two) * jnp.mean(resid * scaled_two, axis=1, keepdims=True)
    )
    grad_gain_two = jnp.sum(d_h_two * resid * r_two, axis=0)

    d_branch, grad_up = lax.optimization_barrier((row_major(d_resid.astype(bf16)), grad_up))
    d_branch = row_major(lax.all_gather(d_branch, "seq", axis=0, tiled=True))
    up_near = [sent(grad_up, k) for k in near]
    up_near, (d_branch, grad_up, outs[1]) = together(up_near, [d_branch, grad_up, outs[1]])
    up_back = dict(zip(near, up_near))
    up_far = [sent(grad_up, k) for k in far]
    d_att = contract_last(d_branch, wo_own).astype(bf16)
    grad_wo = contract_first(attended, d_branch).astype(bf16).reshape(F, sub, D)
    wo_back = return_heads(row_major(grad_wo), s, S, F)
    d_raw, d_sinks = attend_back(boundary, sinks, queries, kv, d_att, lse, cosine, sine)
    up_far, wo_back, (d_raw, outs[1]) = together(up_far, wo_back, [d_raw, outs[1]])
    up_back.update(zip(far, up_far))
    grad_wo = return_places(wo_back, s)
    wo_got = [sent(grad_wo, k) for k in range(1, F)]
    d_h_part, grad_gain_one = rows_back(d_raw, w_qkv, x_all, r_one_all)
    d_raw, d_h_part = lax.optimization_barrier((d_raw, d_h_part))
    d_h_one = lax.psum_scatter(d_h_part, "seq", scatter_dimension=0, tiled=True)
    grad_qkv = contract_first(h_one, d_raw).astype(bf16)
    grad_qkv = row_major(grad_qkv).reshape(F, rows_d, q_cols + 2 * head_dim)
    grad_expert_in = join_units(placed_parts(grad_gate, gate_back), placed_parts(grad_up, up_back), ff)[None]
    mix_second = spread_sum(outs[1])
    wo_got, mix_second, (grad_qkv, grad_expert_in) = together(
        wo_got, mix_second, [grad_qkv, grad_expert_in]
    )
    qkv_got = [sent(grad_qkv, k) for k in range(1, F)]
    qkv_got[0], d_sinks, grad_gain_one, grad_gain_two, grad_router = lax.optimization_barrier(
        (qkv_got[0], d_sinks, grad_gain_one, grad_gain_two, grad_router)
    )
    qkv_got[0], *mix_first = lax.optimization_barrier((qkv_got[0], *mix_first))
    grad_wo = summed_parts(grad_wo, wo_got).astype(bf16)
    grad_output = row_major(lax.all_gather(row_major(grad_wo), "seq", axis=0, tiled=True))
    grad_output = grad_output.astype(f32)
    mixed = sum(piece.astype(f32) for piece in mix_first).astype(bf16)
    mix_got = [shifted(mixed[k], "fsdp", -k) for k in range(1, half)]
    own_heads = jnp.zeros((heads,), f32)
    own_heads = lax.dynamic_update_slice_in_dim(own_heads, d_sinks[0, :heads_own], s * heads_own, 0)
    tiny = jnp.concatenate(
        [
            grad_gain_one[0].reshape(F, rows_d),
            grad_gain_two.reshape(F, rows_d),
            own_heads.reshape(F, own_sinks),
            grad_router.reshape(F, rows_d * experts),
        ],
        axis=1,
    )
    tiny = jnp.pad(tiny, ((0, 0), (0, round_up(cut[3], 16 * LANES) - cut[3]))).reshape(F, -1, LANES)
    tiny = sum_direct(tiny, "fsdp")
    d_h_one = d_h_one.astype(f32)
    r_one = lax.rsqrt(jnp.mean(x_f * x_f, axis=1, keepdims=True) + norm_eps)
    scaled_one = g_one * d_h_one
    input_grad = (
        d_resid
        + r_one * scaled_one
        - x_f * (r_one * r_one * r_one) * jnp.mean(x_f * scaled_one, axis=1, keepdims=True)
    )
    qkv_got, mix_got, (input_grad, tiny, grad_output) = together(
        qkv_got, mix_got, [input_grad, tiny, grad_output]
    )
    grad_qkv = summed_parts(grad_qkv, qkv_got).astype(bf16)
    grad_qkv = lax.all_gather(grad_qkv, "seq", axis=0)
    tiny = jnp.sum(gather_direct(tiny, "seq"), axis=0).reshape(-1)
    grad_query, grad_key, grad_value = join_heads(grad_qkv, q_cols, head_dim, kv_heads)

    mixture = mixed[0].astype(f32)
    mixed = sum(piece.astype(f32) for piece in mix_second).astype(bf16)
    for piece in mix_got + [shifted(mixed[k], "fsdp", -half - k) for k in range(half)]:
        mixture = mixture + piece.astype(f32)
    block_out = (resid + mixture[:, :D]).astype(bf16)

    return (
        block_out[None],
        input_grad[None],
        tiny[: cut[0]],
        grad_query,
        grad_key,
        grad_value,
        grad_output,
        tiny[cut[1] : cut[2]],
        tiny[cut[0] : cut[1]],
        tiny[cut[2] : cut[3]].reshape(rows_d, experts),
        grad_expert_in,
        grad_down[None],
    )


def solution(mesh):
    tokens = P("fsdp", "seq", None)
    vector = P("fsdp")
    matrix = P("fsdp", None)
    expert = P("seq", "fsdp", None)
    return jax.shard_map(
        local,
        mesh=mesh,
        in_specs=(
            tokens, tokens, vector, tokens, vector, matrix, matrix, matrix, matrix, vector, vector, matrix, expert, expert,
        ),
        out_specs=(
            tokens, tokens, vector, matrix, matrix, matrix, matrix, vector, vector, matrix, expert, expert,
        ),
        check_vma=False,
    )
```
